256 devices in a mesh: row: 16 (over y, x), col: 16 (over z, core).
Axes of the slice: x: 4, y: 4, z: 8, core: 2. Of those that a mesh axis runs over, the one named last changes fastest.
Arguments:
- term_matrix: bfloat16 [12288, 32768], P('row', 'col'), may hold values from -6 to 6
- sign_bits: int32 [32768], P('col'), may hold values from 0 to 1
- sampled: int32 [256, 512], P('col'), may hold values from 0 to 127
Outputs:
- projected: float32 [512, 32768], P('row', 'col')
The draws below stay inside these ranges and needn't reach their ends.
All inputs are finite; a program needn't handle non-finite values.
Results may differ from the reference program's by a relative error of at most 0.0025.
Values may be sent and summed in bfloat16 or wider, within the bound.
A program may use at most 64 MiB of HBM per device.

```python
import jax
import jax.numpy as jnp
from jax import lax

SKETCH = 512
ROWS = 12288
COLS = 32768
NBLK = 256


def with_ends(values, own_key, least, top_value):
    extent = values.shape
    spot = [jax.random.randint(jax.random.fold_in(own_key, axis), (), 0, extent[axis]) for axis in range(len(extent))]
    values = values.at[tuple(spot)].set(least)
    longest = extent.index(max(extent))
    spot[longest] = (spot[longest] + 1) % extent[longest]
    return values.at[tuple(spot)].set(top_value)


def shard_levels(key, extent, pieces, low, high):
    def one(position, blocks):
        draws = jax.random.uniform(jax.random.fold_in(jax.random.fold_in(key, 6), position), (blocks,), jnp.float32, low / len(pieces), high / len(pieces))
        return jnp.repeat(jnp.exp(draws), extent[position] // blocks).reshape((-1,) + (1,) * (len(extent) - position - 1))

    loudness = one(*pieces[0])
    for cut in pieces[1:]:
        loudness = loudness * one(*cut)
    return loudness


def bell_draw(key, extent, scale, bound, shards=(), kind=jnp.bfloat16):
    entries = jax.random.normal(key, extent, jnp.float32) * scale
    if len(shards) > 0:
        entries = shard_levels(key, extent, shards, -0.22, 0.18) * entries
    return jnp.clip(entries, min=-bound, max=bound).astype(kind)


def setup_inputs(seed: int = 0) -> dict:
    key_list = jax.random.split(jax.random.key(seed), 4)
    term_matrix = bell_draw(key_list[0], (ROWS, COLS), 1.0, 6.0, ((0, 16), (1, 16)))
    sign_bits = with_ends(jax.random.randint(key_list[1], (COLS,), 0, 2), jax.random.fold_in(key_list[1], 1), 0, 1).astype(jnp.int32)
    sampled = with_ends(jax.random.randint(key_list[2], (NBLK, SKETCH), 0, 128), jax.random.fold_in(key_list[2], 1), 0, 127).astype(jnp.int32)
    return dict(term_matrix=term_matrix, sign_bits=sign_bits, sampled=sampled)


def bit_parity(value):
    total = jnp.zeros_like(value)
    for bit_pos in range(7):
        total = total + (value >> bit_pos & 1)
    return total & 1

def hadamard_cols(sign_part, sample_part):
    blocks = sample_part.shape[0]
    hrange = lax.iota(jnp.int32, 128)
    parity = bit_parity(hrange[None, :, None] & sample_part[:, None, :])
    values = (1 - 2 * parity) * (2 * sign_part.reshape(blocks, 128, 1) - 1)
    return values.reshape(blocks * 128, sample_part.shape[1]).astype(jnp.bfloat16)

def sketch_block(a_rows, sign_bits, sampled):
    group_cols = min(1024, a_rows.shape[1])
    groups = a_rows.shape[1] // group_cols
    per_group = group_cols // 128

    def advance(running, group_idx):
        a_part = lax.dynamic_slice_in_dim(a_rows, group_idx * group_cols, group_cols, 1)
        sign_part = lax.dynamic_slice_in_dim(sign_bits, group_idx * group_cols, group_cols, 0)
        sample_part = lax.dynamic_slice_in_dim(sampled, group_idx * per_group, per_group, 0)
        sketch_cols = hadamard_cols(sign_part, sample_part)
        return (running + jnp.dot(a_part.astype(jnp.float32), sketch_cols.astype(jnp.float32), preferred_element_type=jnp.float32), None)
    start_sum = jnp.zeros((a_rows.shape[0], sampled.shape[1]), jnp.float32)
    running, ignored = lax.scan(advance, start_sum, jnp.arange(groups, dtype=jnp.int32))
    return running

def reference(term_matrix, sign_bits, sampled):
    sketch = sketch_block(term_matrix, sign_bits, sampled)
    basis, upper = jnp.linalg.qr(sketch)
    signs_diag = jnp.sign(jnp.diagonal(upper))
    basis = (basis * signs_diag[None, :]).astype(jnp.bfloat16)
    return jnp.dot(basis.T.astype(jnp.float32), term_matrix.astype(jnp.float32), preferred_element_type=jnp.float32)
```

```python
import jax
import jax.numpy as jnp
from jax import lax
from jax.experimental import pallas as pl
from jax.experimental.pallas import tpu as pltpu
from jax.sharding import PartitionSpec as P

MESH = pl.DeviceIdType.MESH
HI = lax.Precision.HIGHEST
F32 = jnp.float32
BF16 = jnp.bfloat16
STRIPS = 4
LN2 = 0.6931471805599453


def barrier(targets):
    sem = pltpu.get_barrier_semaphore()
    for target in targets:
        pl.semaphore_signal(sem, inc=1, device_id=target, device_id_type=MESH)
    return lambda: pl.semaphore_wait(sem, len(targets))


def send(src, dst, send_sem, recv_sem, target):
    copy = pltpu.make_async_remote_copy(
        src_ref=src, dst_ref=dst, send_sem=send_sem, recv_sem=recv_sem, device_id=target, device_id_type=MESH
    )
    copy.start()
    return copy


def pack(value):
    top = jnp.max(jnp.max(jnp.abs(value), axis=0, keepdims=True), axis=1, keepdims=True)
    power = jnp.ceil(jnp.log(jnp.maximum(top, 1e-30)) * (1.0 / LN2)) - 14.0
    coded = jnp.floor(value * jnp.exp(power * -LN2) + 0.5).astype(jnp.int32).astype(jnp.int16)
    return coded, jnp.broadcast_to(power, (16, 128)).astype(jnp.int32).astype(jnp.int16)


def step_of(power):
    return jnp.exp(power.astype(jnp.int32).astype(F32) * LN2)[0:1, :]


def sketch_kernel(
    a_ref, sign_ref, samp_ref, y_ref, om, mate_out, mate_in, own, part_out, part_in, full, s_mate, r_mate, s_part, r_part, s_full, r_full, s_fwd, r_fwd
):
    row, col = lax.axis_index("row"), lax.axis_index("col")
    z, core = col // 2, lax.rem(col, 2)
    mate = (row, 2 * z + 1 - core)

    def chip(distance):
        return (row, 2 * lax.rem(z + distance, 8) + core)

    ready = barrier([mate] + [chip(d) for d in range(1, 8)])

    def make_block(block, carry):
        term = lax.broadcasted_iota(jnp.int32, (128, 512), 0)
        parity = lax.population_count(term & samp_ref[block]) & 1
        om[pl.ds(pl.multiple_of(block * 128, 128), 128), :] = (1 - 2 * parity).astype(F32).astype(BF16)
        return carry

    lax.fori_loop(0, 16, make_block, 0)
    signs = (2 * sign_ref[...] - 1).astype(F32).astype(BF16)

    def half(which, out):
        rows = a_ref[pl.ds(pl.multiple_of(which * 384, 384), 384), :] * signs
        for n in range(2):
            out(n, jnp.dot(rows, om[:, 256 * n : 256 * n + 256], preferred_element_type=F32))

    mate_copies = []

    def to_mate(n, value):
        mate_out[n] = value
        if n == 0:
            ready()
        mate_copies.append(send(mate_out.at[n], mate_in.at[n], s_mate.at[n], r_mate.at[n], mate))

    def keep(n, value):
        own[:, 256 * n : 256 * n + 256] = value

    half(1 - core, to_mate)
    half(core, keep)
    for n in range(2):
        mate_copies[n].wait_recv()
        own[:, 256 * n : 256 * n + 256] += mate_in[n]

    part_copies = []
    for d in (4, 3, 5, 2, 6, 1, 7):
        there = lax.rem(z + d, 8)
        coded, power = pack(own[pl.ds(pl.multiple_of(there * 48, 48), 48), :])
        for j in range(4):
            part_out[d, 48 * j : 48 * j + 48, :] = coded[:, 128 * j : 128 * j + 128]
        part_out[d, 192:208, :] = power
        part_copies.append(send(part_out.at[d], part_in.at[d], s_part.at[d], r_part.at[d], chip(d)))
    for copy in part_copies:
        copy.wait_recv()
    slot = core * 8 + z
    scales = [step_of(part_in[d, 192:208, :]) for d in range(1, 8)]
    for j in range(4):
        total = own[pl.ds(pl.multiple_of(z * 48, 48), 48), 128 * j : 128 * j + 128]
        for d in range(1, 8):
            total = total + part_in[d, 48 * j : 48 * j + 48, :].astype(jnp.int32).astype(F32) * scales[d - 1]
        full[slot, :, 128 * j : 128 * j + 128] = total.astype(BF16)

    full_copies = []
    for d in (4, 3, 5, 2, 6, 1, 7):
        full_copies.append((d, send(full.at[slot], full.at[slot], s_full.at[d], r_full.at[d], chip(d))))
    fwd_copies = [send(full.at[slot], full.at[slot], s_fwd.at[0], r_fwd.at[0], mate)]
    for d, copy in reversed(full_copies):
        copy.wait_recv()
        came = core * 8 + lax.rem(z + 8 - d, 8)
        fwd_copies.append(send(full.at[came], full.at[came], s_fwd.at[d], r_fwd.at[d], mate))
    for copy in fwd_copies:
        copy.wait_recv()
    for s in range(16):
        y_ref[48 * s : 48 * s + 48, :] = full[s]
    for copy in mate_copies + part_copies + [c for _, c in full_copies] + fwd_copies:
        copy.wait_send()


def sketch(term_matrix, sign_bits, sampled):
    vmem = pl.BlockSpec(memory_space=pltpu.VMEM)
    return pl.pallas_call(
        sketch_kernel,
        out_shape=jax.ShapeDtypeStruct((768, 512), BF16),
        in_specs=[vmem, vmem, vmem],
        out_specs=vmem,
        scratch_shapes=[
            pltpu.VMEM((2048, 512), BF16),
            pltpu.VMEM((2, 384, 256), F32),
            pltpu.VMEM((2, 384, 256), F32),
            pltpu.VMEM((384, 512), F32),
            pltpu.VMEM((8, 208, 128), jnp.int16),
            pltpu.VMEM((8, 208, 128), jnp.int16),
            pltpu.VMEM((16, 48, 512), BF16),
            pltpu.SemaphoreType.DMA((2,)),
            pltpu.SemaphoreType.DMA((2,)),
            pltpu.SemaphoreType.DMA((8,)),
            pltpu.SemaphoreType.DMA((8,)),
            pltpu.SemaphoreType.DMA((8,)),
            pltpu.SemaphoreType.DMA((8,)),
            pltpu.SemaphoreType.DMA((8,)),
            pltpu.SemaphoreType.DMA((8,)),
        ],
        compiler_params=pltpu.CompilerParams(collective_id=0, has_side_effects=True, vmem_limit_bytes=48 << 20),
    )(term_matrix, sign_bits.reshape(1, 2048), sampled.reshape(16, 1, 512))


def lane_of(x, lane):
    return jnp.broadcast_to(x[:, lane : lane + 1], (8, 128))


def dot_t(a, b):
    return lax.dot_general(a, b, (((0,), (0,)), ((), ())), precision=HI, preferred_element_type=F32)


def dot_hi(a, b):
    return jnp.dot(a, b, precision=HI, preferred_element_type=F32)


def factor_block(x, w, base):
    for t in range(16):
        at = 8 * t
        strip = x[t, :, 0:128]
        for j in range(8):
            x[20 + j // 2, :, 128 * (j % 2) : 128 * (j % 2) + 128] = lane_of(strip, at + j)
        left = [jnp.broadcast_to(x[t, i : i + 1, 0:128], (8, 128)) for i in range(8)]
        right = [jnp.broadcast_to(x[t, i : i + 1, 128:256], (8, 128)) for i in range(8)]
        a = [[None] * 8 for _ in range(8)]
        for i in range(8):
            for j in range(i, 8):
                a[i][j] = jnp.broadcast_to(x[20 + j // 2, i : i + 1, 128 * (j % 2) : 128 * (j % 2) + 128], (8, 128))
        recips, mult = [], [[None] * 8 for _ in range(8)]
        for k in range(8):
            recips.append(1.0 / a[k][k])
            for j in range(k + 1, 8):
                mult[k][j] = a[k][j] * recips[k]
            for i in range(k + 1, 8):
                for j in range(i, 8):
                    a[i][j] = a[i][j] - mult[k][i] * a[k][j]
            for j in range(k + 1, 8):
                left[j] = left[j] - mult[k][j] * left[k]
                right[j] = right[j] - mult[k][j] * right[k]
        last = STRIPS * (t // STRIPS) + STRIPS
        for k in range(8):
            scale = lax.rsqrt(a[k][k])
            w[base // 8 + t, k : k + 1, :] = (right[k] * scale)[0:1]
            if last < 16:
                x[16 + t % STRIPS, k : k + 1, 0:128] = (left[k] * scale)[0:1]
                x[16 + t % STRIPS, k : k + 1, 128:256] = (right[k] * scale)[0:1]
        if t + 1 < last:
            v_left, v_right = [None] * 8, [None] * 8
            for i in range(7, -1, -1):
                vl, vr = left[i] * recips[i], right[i] * recips[i]
                for j in range(7, i, -1):
                    vl = vl - mult[i][j] * v_left[j]
                    vr = vr - mult[i][j] * v_right[j]
                v_left[i], v_right[i] = vl, vr
            for s in range(t + 1, last):
                old = x[s, :, 0:128]
                new_left, new_right = old, x[s, :, 128:256]
                for k in range(8):
                    c = lane_of(old, at + k)
                    new_left = new_left - c * v_left[k]
                    new_right = new_right - c * v_right[k]
                x[s, :, 0:128] = new_left
                x[s, :, 128:256] = new_right
        elif last < 16:
            u = x[16 : 16 + STRIPS].reshape(8 * STRIPS, 256)
            change = dot_t(u[:, 0:128], u)
            x[last:16] = x[last:16] - change[8 * last :].reshape(16 - last, 8, 256)


def factor(g, x, w):
    eye = (lax.broadcasted_iota(jnp.int32, (128, 128), 0) == lax.broadcasted_iota(jnp.int32, (128, 128), 1)).astype(F32)

    def step(k, carry):
        x[0:16, :, 0:128] = g[5 * k].reshape(16, 8, 128)
        x[0:16, :, 128:256] = eye.reshape(16, 8, 128)
        factor_block(x, w, 128 * k)
        inverse = w[pl.ds(16 * k, 16)].reshape(128, 128)

        def panel(j, c):
            g[4 * k + j] = dot_hi(inverse, g[4 * k + j])
            return c

        lax.fori_loop(k + 1, 4, panel, 0)

        def outer(i, c):
            left = g[4 * k + i]

            def inner(j, cc):
                g[4 * i + j] = g[4 * i + j] - dot_t(left, g[4 * k + j])
                return cc

            return lax.fori_loop(i, 4, inner, c)

        lax.fori_loop(k + 1, 4, outer, 0)
        return carry

    lax.fori_loop(0, 4, step, 0)


TRI = [(i, j) for i in range(4) for j in range(i, 4)]


def project_kernel(
    a_ref, y_ref, o_ref, yt, gloc, gin, gfull, gsq, x, w, zf, zout, zin, pbuf, obuf,
    s_c, r_c, s_d, r_d, s_e, r_e, s_z, r_z, s_o, r_o,
):
    row, col = lax.axis_index("row"), lax.axis_index("col")
    core = lax.rem(col, 2)
    mate = (row, col + 1 - 2 * core)

    def peer(d):
        return lax.rem(row + d, 16)

    def piece(r):
        return pl.ds(pl.multiple_of(40 * (2 * r + core), 8), 40)

    ready = barrier([mate] + [(peer(d), col) for d in range(1, 16)])
    for i in range(4):
        yt[128 * i : 128 * i + 128, :] = y_ref[:, 128 * i : 128 * i + 128].T
    at = 0
    for i in range(4):
        blocks = jnp.dot(yt[128 * i : 128 * i + 128, :], y_ref[:, 128 * i :], preferred_element_type=F32)
        for j in range(4 - i):
            gloc[at : at + 128, :] = blocks[:, 128 * j : 128 * j + 128]
            at += 128
    ready()
    c_copies = []
    for d in range(1, 16):
        c_copies.append(send(gloc.at[piece(peer(d))], gin.at[d], s_c.at[d], r_c.at[d], (peer(d), col)))

    def product(n, carry):
        cols = pl.ds(pl.multiple_of(256 * n, 256), 256)
        zf[:, cols] = jnp.dot(yt[...], a_ref[:, cols], preferred_element_type=F32)
        return carry

    lax.fori_loop(0, 8, product, 0)

    def code(d, carry):
        cols = pl.ds(pl.multiple_of(128 * peer(d), 128), 128)
        coded, power = pack(zf[:, cols])
        zout[d, 0:512, :] = coded
        zout[d, 512:528, :] = power
        return carry

    lax.fori_loop(1, 16, code, 0)

    for copy in c_copies:
        copy.wait_recv()
    total = gloc[piece(row), :]
    for d in range(1, 16):
        total = total + gin[d]
    gfull[piece(row), :] = total
    d_copies, e_copies, z_copies = [], [], []
    for d in range(1, 16):
        d_copies.append(send(gfull.at[piece(row)], gfull.at[piece(row)], s_d.at[d], r_d.at[d], (peer(d), col)))
    e_copies.append(send(gfull.at[piece(row)], gfull.at[piece(row)], s_e.at[0], r_e.at[0], mate))
    for d in range(1, 16):
        z_copies.append(send(zout.at[d], zin.at[d], s_z.at[d], r_z.at[d], (peer(d), col)))
    for d in range(1, 16):
        d_copies[d - 1].wait_recv()
        came = lax.rem(row + 16 - d, 16)
        e_copies.append(send(gfull.at[piece(came)], gfull.at[piece(came)], s_e.at[d], r_e.at[d], mate))
    for copy in e_copies:
        copy.wait_recv()
    for n, (i, j) in enumerate(TRI):
        gsq[4 * i + j] = gfull[128 * n : 128 * n + 128, :]

    factor(gsq, x, w)

    for copy in z_copies:
        copy.wait_recv()

    def solve(k, carry):
        rows = pl.ds(pl.multiple_of(128 * k, 128), 128)
        value = zf[rows, pl.ds(pl.multiple_of(128 * row, 128), 128)]

        def add(d, v):
            return v + zin[d, rows, :].astype(jnp.int32).astype(F32) * step_of(zin[d, 512:528, :])

        value = lax.fori_loop(1, 16, add, value)

        def less(j, v):
            return v - dot_t(gsq[4 * j + k], pbuf[pl.ds(pl.multiple_of(128 * j, 128), 128), :])

        value = lax.fori_loop(0, k, less, value)
        pbuf[rows, :] = dot_hi(w[pl.ds(16 * k, 16)].reshape(128, 128), value)
        return carry

    lax.fori_loop(0, 4, solve, 0)

    o_copies = []
    for d in range(1, 16):
        part = pl.ds(pl.multiple_of(32 * peer(d), 32), 32)
        o_copies.append(send(pbuf.at[part], obuf.at[row], s_o.at[d], r_o.at[d], (peer(d), col)))
    obuf[row] = pbuf[pl.ds(pl.multiple_of(32 * row, 32), 32), :]
    for copy in o_copies:
        copy.wait_recv()
    for r in range(16):
        o_ref[:, 128 * r : 128 * r + 128] = obuf[r]
    for copy in c_copies + d_copies + e_copies + z_copies + o_copies:
        copy.wait_send()


def project(term_matrix, basis):
    vmem = pl.BlockSpec(memory_space=pltpu.VMEM)
    return pl.pallas_call(
        project_kernel,
        out_shape=jax.ShapeDtypeStruct((32, 2048), F32),
        in_specs=[vmem, vmem],
        out_specs=vmem,
        scratch_shapes=[
            pltpu.VMEM((512, 768), BF16),
            pltpu.VMEM((1280, 128), F32),
            pltpu.VMEM((16, 40, 128), F32),
            pltpu.VMEM((1280, 128), F32),
            pltpu.VMEM((16, 128, 128), F32),
            pltpu.VMEM((24, 8, 256), F32),
            pltpu.VMEM((64, 8, 128), F32),
            pltpu.VMEM((512, 2048), F32),
            pltpu.VMEM((16, 528, 128), jnp.int16),
            pltpu.VMEM((16, 528, 128), jnp.int16),
            pltpu.VMEM((512, 128), F32),
            pltpu.VMEM((16, 32, 128), F32),
        ]
        + [pltpu.SemaphoreType.DMA((16,))] * 10,
        compiler_params=pltpu.CompilerParams(collective_id=1, has_side_effects=True, vmem_limit_bytes=48 << 20),
    )(term_matrix, basis)


def shards(term_matrix, sign_bits, sampled):
    return project(term_matrix, sketch(term_matrix, sign_bits, sampled))


def solution(mesh):
    in_specs = (P("row", "col"), P("col"), P("col", None))
    return jax.shard_map(shards, mesh=mesh, in_specs=in_specs, out_specs=P("row", "col"), check_vma=False)
```

```python
import jax
import jax.numpy as jnp
from jax import lax
from jax.experimental import pallas as pl
from jax.experimental.pallas import tpu as pltpu
from jax.sharding import PartitionSpec as P

MESH = pl.DeviceIdType.MESH
F32 = jnp.float32
BF16 = jnp.bfloat16
STRIPS = 4
LN2 = 0.6931471805599453


def barrier(targets):
    sem = pltpu.get_barrier_semaphore()
    for target in targets:
        pl.semaphore_signal(sem, inc=1, device_id=target, device_id_type=MESH)
    return lambda: pl.semaphore_wait(sem, len(targets))


def send(src, dst, send_sem, recv_sem, target):
    copy = pltpu.make_async_remote_copy(
        src_ref=src, dst_ref=dst, send_sem=send_sem, recv_sem=recv_sem, device_id=target, device_id_type=MESH
    )
    copy.start()
    return copy


def pack(value):
    top = jnp.max(jnp.max(jnp.abs(value), axis=0, keepdims=True), axis=1, keepdims=True)
    power = jnp.ceil(jnp.log(jnp.maximum(top, 1e-30)) * (1.0 / LN2)) - 14.0
    coded = jnp.floor(value * jnp.exp(power * -LN2) + 0.5).astype(jnp.int32).astype(jnp.int16)
    return coded, jnp.broadcast_to(power, (16, 128)).astype(jnp.int32).astype(jnp.int16)


def step_of(power):
    return jnp.exp(power.astype(jnp.int32).astype(F32) * LN2)[0:1, :]


def lane_of(x, lane):
    return jnp.broadcast_to(x[:, lane : lane + 1], (8, 128))


def split(u):
    high = u.astype(BF16)
    rest = u - high.astype(F32)
    mid = rest.astype(BF16)
    return high, mid, (rest - mid.astype(F32)).astype(BF16)


def dot_t(a, b):
    ah, am, al = split(a)
    bh, bm, bl = split(b)
    left = jnp.concatenate([ah, ah, am, ah, am, al], 0)
    right = jnp.concatenate([bh, bm, bh, bl, bm, bh], 0)
    return lax.dot_general(left, right, (((0,), (0,)), ((), ())), preferred_element_type=F32)


def dot_hi(a, b):
    ah, am, al = split(a)
    bh, bm, bl = split(b)
    left = jnp.concatenate([ah, ah, am, ah, am, al], 1)
    right = jnp.concatenate([bh, bm, bh, bl, bm, bh], 0)
    return jnp.dot(left, right, preferred_element_type=F32)


def factor_block(x, w, base):
    lanes = lax.broadcasted_iota(jnp.int32, (8, 128), 1)
    for t in range(16):
        at = 8 * t
        strip = x[t]
        for j in range(8):
            x[24 + j] = lane_of(strip, at + j)
        here = (lanes >= at) & (lanes < at + 8)
        a = [[None] * 8 for _ in range(8)]
        for i in range(8):
            for j in range(i, 8):
                a[i][j] = jnp.broadcast_to(x[24 + j, i : i + 1, :], (8, 128))
        rows = [jnp.where(here, (lanes == at + i).astype(F32), jnp.broadcast_to(x[t, i : i + 1, :], (8, 128))) for i in range(8)]
        recips, mult = [], [[None] * 8 for _ in range(8)]
        for k in range(8):
            recips.append(1.0 / a[k][k])
            for j in range(k + 1, 8):
                mult[k][j] = a[k][j] * recips[k]
            for i in range(k + 1, 8):
                for j in range(i, 8):
                    a[i][j] = a[i][j] - mult[k][i] * a[k][j]
            for j in range(k + 1, 8):
                rows[j] = rows[j] - mult[k][j] * rows[k]
        last = STRIPS * (t // STRIPS) + STRIPS
        done = lanes < at + 8
        for k in range(8):
            u = rows[k] * lax.rsqrt(a[k][k])
            w[base // 8 + t, k : k + 1, :] = jnp.where(done, u, 0.0)[0:1]
            if last < 16:
                x[16 + t % STRIPS, k : k + 1, :] = jnp.where(done | (lanes >= 8 * last), u, 0.0)[0:1]
        if t + 1 < last:
            v = [None] * 8
            for i in range(7, -1, -1):
                v[i] = rows[i] * recips[i]
                for j in range(7, i, -1):
                    v[i] = v[i] - mult[i][j] * v[j]
            for s in range(t + 1, last):
                old = x[s]
                new = jnp.where(here, 0.0, old)
                for k in range(8):
                    new = new - lane_of(old, at + k) * v[k]
                x[s] = new
        elif last < 16:
            u = x[16 : 16 + STRIPS].reshape(8 * STRIPS, 128)
            change = dot_t(u, u)[8 * last :].reshape(16 - last, 8, 128)
            inside = (lanes >= 8 * (last - STRIPS)) & (lanes < 8 * last)
            x[last:16] = jnp.where(inside[None], 0.0, x[last:16]) - change


def factor(g, x, w, between):
    def step(k, carry):
        between(k)
        x[0:16] = g[5 * k].reshape(16, 8, 128)
        factor_block(x, w, 128 * k)
        inverse = w[pl.ds(16 * k, 16)].reshape(128, 128)

        def panel(j, c):
            g[4 * k + j] = dot_hi(inverse, g[4 * k + j])
            return c

        lax.fori_loop(k + 1, 4, panel, 0)

        def outer(i, c):
            left = g[4 * k + i]

            def inner(j, cc):
                g[4 * i + j] = g[4 * i + j] - dot_t(left, g[4 * k + j])
                return cc

            return lax.fori_loop(i, 4, inner, c)

        lax.fori_loop(k + 1, 4, outer, 0)
        return carry

    lax.fori_loop(0, 4, step, 0)


TRI = [(i, j) for i in range(4) for j in range(i, 4)]
FAR_FIRST = (4, 3, 5, 2, 6, 1, 7)
NEAR_FIRST = FAR_FIRST[::-1]
MID = 2


def kernel(
    a_hbm, sign_ref, samp_ref, o_ref,
    a, om, mate_out, mate_in, own, part_out, part_in, full, yt, gloc, gin, gfull, gsq, x, w,
    zf, zs1, zr1, zs2, zr2, zown, pbuf, obuf,
    s_a, s_mate, r_mate, s_part, r_part, s_full, r_full, s_fwd, r_fwd,
    s_c, r_c, s_d, r_d, s_e, r_e, s_z1, r_z1, s_z2, r_z2, s_o, r_o,
):
    row, col = lax.axis_index("row"), lax.axis_index("col")
    z, core = col // 2, lax.rem(col, 2)
    py, px = row // 4, lax.rem(row, 4)
    mate = (row, 2 * z + 1 - core)

    def chip(distance):
        return (row, 2 * lax.rem(z + distance, 8) + core)

    def peer(d):
        return lax.rem(row + d, 16)

    def half_rows(which):
        return pl.ds(pl.multiple_of(which * 384, 384), 384)

    loads = []
    for n, which in enumerate((1 - core, core)):
        loads.append(pltpu.make_async_copy(a_hbm.at[half_rows(which)], a.at[half_rows(which)], s_a.at[n]))
        loads[n].start()
    ready = barrier([mate] + [chip(d) for d in range(1, 8)] + [(peer(d), col) for d in range(1, 16)])

    term = lax.broadcasted_iota(jnp.int32, (128, 512), 0)
    for block in range(16):
        parity = lax.population_count(term & samp_ref[block : block + 1, :]) & 1
        om[128 * block : 128 * block + 128, :] = (1 - 2 * parity).astype(F32).astype(BF16)
    signs = (2 * sign_ref[...] - 1).astype(F32).astype(BF16)

    def partial(which, n):
        rows = a[half_rows(which), :] * signs
        return jnp.dot(rows, om[:, 256 * n : 256 * n + 256], preferred_element_type=F32)

    mate_copies, part_copies, full_copies, fwd_copies = [], [], [], []
    loads[0].wait()
    for n in range(2):
        mate_out[n] = partial(1 - core, n)
        if n == 0:
            ready()
        mate_copies.append(send(mate_out.at[n], mate_in.at[n], s_mate.at[n], r_mate.at[n], mate))
    loads[1].wait()
    for n in range(2):
        own[n] = partial(core, n)
        mate_copies[n].wait_recv()
        own[n] += mate_in[n]
        for d in FAR_FIRST:
            there = lax.rem(z + d, 8)
            coded, power = pack(own[n, pl.ds(pl.multiple_of(there * 48, 48), 48), :])
            part_out[n, d, 0:48, :] = coded[:, 0:128]
            part_out[n, d, 48:96, :] = coded[:, 128:256]
            part_out[n, d, 96:112, :] = power
            part_copies.append(send(part_out.at[n, d], part_in.at[n, d], s_part.at[n, d], r_part.at[n, d], chip(d)))
    slot = core * 8 + z
    for n in range(2):
        for copy in part_copies[7 * n : 7 * n + 7]:
            copy.wait_recv()
        for j in range(2):
            total = own[n, pl.ds(pl.multiple_of(z * 48, 48), 48), 128 * j : 128 * j + 128]
            for d in range(1, 8):
                value = part_in[n, d, 48 * j : 48 * j + 48, :].astype(jnp.int32).astype(F32)
                total = total + value * step_of(part_in[n, d, 96:112, :])
            full[n, slot, :, 128 * j : 128 * j + 128] = total.astype(BF16)
        mine = full.at[n, slot]
        for d in FAR_FIRST:
            full_copies.append(send(mine, mine, s_full.at[n, d], r_full.at[n, d], chip(d)))
        fwd_copies.append(send(mine, mine, s_fwd.at[n, 0], r_fwd.at[n, 0], mate))
    for n in range(2):
        for m, d in enumerate(FAR_FIRST):
            full_copies[7 * n + m].wait_recv()
            came = full.at[n, core * 8 + lax.rem(z + 8 - d, 8)]
            fwd_copies.append(send(came, came, s_fwd.at[n, d], r_fwd.at[n, d], mate))
    for copy in fwd_copies:
        copy.wait_recv()

    def piece(r):
        return pl.ds(pl.multiple_of(40 * (2 * r + core), 8), 40)

    for i in range(4):
        yt[128 * i : 128 * i + 128, :] = full[i // 2, :, :, 128 * (i % 2) : 128 * (i % 2) + 128].reshape(768, 128).T
    for i in range(4):
        for n in range(i // 2, 2):
            blocks = jnp.dot(yt[128 * i : 128 * i + 128, :], full[n].reshape(768, 256), preferred_element_type=F32)
            for j in range(2 * n, 2 * n + 2):
                if j >= i:
                    at = 128 * TRI.index((i, j))
                    gloc[at : at + 128, :] = blocks[:, 128 * (j - 2 * n) : 128 * (j - 2 * n) + 128]
    c_copies, d_copies, e_copies, o_copies = [], [], [], []
    for d in range(1, 16):
        c_copies.append(send(gloc.at[piece(peer(d))], gin.at[d], s_c.at[d], r_c.at[d], (peer(d), col)))

    def product(n, carry):
        cols = pl.ds(pl.multiple_of(256 * n, 256), 256)
        zf[:, cols] = jnp.dot(yt[...], a[:, cols], preferred_element_type=F32)
        return carry

    lax.fori_loop(0, 8, product, 0)

    def along(h, d, e):
        return (4 * e + lax.rem(px + d, 4)) if h == 0 else (4 * lax.rem(py + d, 4) + e)

    def first(h, d):
        target = (along(h, d, py if h == 0 else px), col)
        return pltpu.make_async_remote_copy(
            src_ref=zs1.at[h, d], dst_ref=zr1.at[h, d], send_sem=s_z1.at[h, d], recv_sem=r_z1.at[h, d], device_id=target, device_id_type=MESH
        )

    def second(h, d):
        target = (along(1 - h, d, px if h == 0 else py), col)
        return pltpu.make_async_remote_copy(
            src_ref=zs2.at[h, d], dst_ref=zr2.at[h, d], send_sem=s_z2.at[h, d], recv_sem=r_z2.at[h, d], device_id=target, device_id_type=MESH
        )

    def z_part(h, r):
        return zf[256 * h : 256 * h + 256, pl.ds(pl.multiple_of(128 * r, 128), 128)]

    for h in range(2):

        def code(m, carry):
            d, e = m // 4 + 1, lax.rem(m, 4)
            coded, power = pack(z_part(h, along(h, d, e)))
            zs1[h, d, e, 0:256, :] = coded
            zs1[h, d, e, 256:272, :] = power
            return carry

        lax.fori_loop(0, 12, code, 0)

    for copy in c_copies:
        copy.wait_recv()
    total = gloc[piece(row), :]
    for d in range(1, 16):
        total = total + gin[d]
    gfull[piece(row), :] = total
    mine = gfull.at[piece(row)]
    for d in range(1, 16):
        d_copies.append(send(mine, mine, s_d.at[d], r_d.at[d], (peer(d), col)))
    e_copies.append(send(mine, mine, s_e.at[0], r_e.at[0], mate))
    for d in (2, 1, 3):
        for h in range(2):
            first(h, d).start()
    for d in range(1, 16):
        d_copies[d - 1].wait_recv()
        came = gfull.at[piece(lax.rem(row + 16 - d, 16))]
        e_copies.append(send(came, came, s_e.at[d], r_e.at[d], mate))
    for copy in e_copies:
        copy.wait_recv()
    for n, (i, j) in enumerate(TRI):
        gsq[4 * i + j] = gfull[128 * n : 128 * n + 128, :]

    def between(k):
        @pl.when(k == MID)
        def _():
            for h in range(2):
                for d in range(1, 4):
                    first(h, d).wait_recv()

                def add(d, carry):
                    e = lax.rem((py if h == 0 else px) + d, 4)
                    value = z_part(h, along(h, 0, e))
                    for f in range(1, 4):
                        step = step_of(zr1[h, f, e, 256:272, :])
                        value = value + zr1[h, f, e, 0:256, :].astype(jnp.int32).astype(F32) * step
                    zown[h, d] = value
                    coded, power = pack(value)
                    zs2[h, d, 0:256, :] = coded
                    zs2[h, d, 256:272, :] = power
                    return carry

                lax.fori_loop(0, 4, add, 0)
                for d in range(1, 4):
                    second(h, d).start()

    factor(gsq, x, w, between)

    for h in range(2):
        for d in range(1, 4):
            second(h, d).wait_recv()
        value = zown[h, 0]
        for d in range(1, 4):
            step = step_of(zr2[h, d, 256:272, :])
            value = value + zr2[h, d, 0:256, :].astype(jnp.int32).astype(F32) * step
        pbuf[256 * h : 256 * h + 256, :] = value
    for k in range(4):
        solved = dot_hi(w[16 * k : 16 * k + 16].reshape(128, 128), pbuf[128 * k : 128 * k + 128, :])
        pbuf[128 * k : 128 * k + 128, :] = solved
        for j in range(k + 1, 4):
            pbuf[128 * j : 128 * j + 128, :] -= dot_t(gsq[4 * k + j], solved)

    for d in range(1, 16):
        part = pl.ds(pl.multiple_of(32 * peer(d), 32), 32)
        o_copies.append(send(pbuf.at[part], obuf.at[row], s_o.at[d], r_o.at[d], (peer(d), col)))
    obuf[row] = pbuf[pl.ds(pl.multiple_of(32 * row, 32), 32), :]
    for copy in o_copies:
        copy.wait_recv()
    for r in range(16):
        o_ref[:, 128 * r : 128 * r + 128] = obuf[r]
    for copy in mate_copies + part_copies + full_copies + fwd_copies + c_copies + d_copies + e_copies + o_copies:
        copy.wait_send()
    for h in range(2):
        for d in range(1, 4):
            first(h, d).wait_send()
            second(h, d).wait_send()


def shards(term_matrix, sign_bits, sampled):
    vmem = pl.BlockSpec(memory_space=pltpu.VMEM)
    dma = pltpu.SemaphoreType.DMA
    return pl.pallas_call(
        kernel,
        out_shape=jax.ShapeDtypeStruct((32, 2048), F32),
        in_specs=[pl.BlockSpec(memory_space=pl.ANY), vmem, vmem],
        out_specs=vmem,
        scratch_shapes=[
            pltpu.VMEM((768, 2048), BF16),
            pltpu.VMEM((2048, 512), BF16),
            pltpu.VMEM((2, 384, 256), F32),
            pltpu.VMEM((2, 384, 256), F32),
            pltpu.VMEM((2, 384, 256), F32),
            pltpu.VMEM((2, 8, 112, 128), jnp.int16),
            pltpu.VMEM((2, 8, 112, 128), jnp.int16),
            pltpu.VMEM((2, 16, 48, 256), BF16),
            pltpu.VMEM((512, 768), BF16),
            pltpu.VMEM((1280, 128), F32),
            pltpu.VMEM((16, 40, 128), F32),
            pltpu.VMEM((1280, 128), F32),
            pltpu.VMEM((16, 128, 128), F32),
            pltpu.VMEM((32, 8, 128), F32),
            pltpu.VMEM((64, 8, 128), F32),
            pltpu.VMEM((512, 2048), F32),
            pltpu.VMEM((2, 4, 4, 272, 128), jnp.int16),
            pltpu.VMEM((2, 4, 4, 272, 128), jnp.int16),
            pltpu.VMEM((2, 4, 272, 128), jnp.int16),
            pltpu.VMEM((2, 4, 272, 128), jnp.int16),
            pltpu.VMEM((2, 4, 256, 128), F32),
            pltpu.VMEM((512, 128), F32),
            pltpu.VMEM((16, 32, 128), F32),
            dma((2,)),
        ]
        + [dma((2,))] * 2
        + [dma((2, 8))] * 6
        + [dma((16,))] * 6
        + [dma((2, 4))] * 4
        + [dma((16,))] * 2,
        compiler_params=pltpu.CompilerParams(collective_id=0, has_side_effects=True, vmem_limit_bytes=48 << 20),
    )(term_matrix, sign_bits.reshape(1, 2048), sampled)


def solution(mesh):
    in_specs = (P("row", "col"), P("col"), P("col", None))
    return jax.shard_map(shards, mesh=mesh, in_specs=in_specs, out_specs=P("row", "col"), check_vma=False)
```

```python
import jax
import jax.numpy as jnp
from jax import lax
from jax.experimental import pallas as pl
from jax.experimental.pallas import tpu as pltpu
from jax.sharding import PartitionSpec as P

MESH = pl.DeviceIdType.MESH
F32 = jnp.float32
BF16 = jnp.bfloat16
STRIPS = 4
LN2 = 0.6931471805599453


def barrier(targets):
    sem = pltpu.get_barrier_semaphore()
    for target in targets:
        pl.semaphore_signal(sem, inc=1, device_id=target, device_id_type=MESH)
    return lambda: pl.semaphore_wait(sem, len(targets))


def send(src, dst, send_sem, recv_sem, target):
    copy = pltpu.make_async_remote_copy(
        src_ref=src, dst_ref=dst, send_sem=send_sem, recv_sem=recv_sem, device_id=target, device_id_type=MESH
    )
    copy.start()
    return copy


def power_of(value):
    top = jnp.max(jnp.max(jnp.abs(value), axis=0, keepdims=True), axis=1, keepdims=True)
    return jnp.ceil(jnp.log(jnp.maximum(top, 1e-30)) * (1.0 / LN2)) - 14.0


def coded(value, power):
    return jnp.floor(value * jnp.exp(power * -LN2) + 0.5).astype(jnp.int32).astype(jnp.int16)


def pack(value, ref, at):
    power = power_of(value)
    ref[at + (slice(0, 256),)] = coded(value, power)
    ref[at + (slice(256, 272),)] = jnp.broadcast_to(power, (16, 128)).astype(jnp.int32).astype(jnp.int16)


def step_of(power):
    return jnp.exp(power.astype(jnp.int32).astype(F32) * LN2)[0:1, :]


def lane_of(x, lane):
    return jnp.broadcast_to(x[:, lane : lane + 1], (8, 128))


def split(u):
    high = u.astype(BF16)
    rest = u - high.astype(F32)
    mid = rest.astype(BF16)
    return high, mid, (rest - mid.astype(F32)).astype(BF16)


def dot_t(a, b):
    ah, am, al = split(a)
    bh, bm, bl = split(b)
    left = jnp.concatenate([ah, ah, am, ah, am, al], 0)
    right = jnp.concatenate([bh, bm, bh, bl, bm, bh], 0)
    return lax.dot_general(left, right, (((0,), (0,)), ((), ())), preferred_element_type=F32)


def dot_hi(a, b):
    ah, am, al = split(a)
    bh, bm, bl = split(b)
    left = jnp.concatenate([ah, ah, am, ah, am, al], 1)
    right = jnp.concatenate([bh, bm, bh, bl, bm, bh], 0)
    return jnp.dot(left, right, preferred_element_type=F32)


def factor_block(x, w, base):
    lanes = lax.broadcasted_iota(jnp.int32, (8, 128), 1)
    for t in range(16):
        at = 8 * t
        strip = x[t]
        for j in range(8):
            x[24 + j] = lane_of(strip, at + j)
        here = (lanes >= at) & (lanes < at + 8)
        a = [[None] * 8 for _ in range(8)]
        for i in range(8):
            for j in range(i, 8):
                a[i][j] = jnp.broadcast_to(x[24 + j, i : i + 1, :], (8, 128))
        rows = [jnp.where(here, (lanes == at + i).astype(F32), jnp.broadcast_to(x[t, i : i + 1, :], (8, 128))) for i in range(8)]
        recips, mult = [], [[None] * 8 for _ in range(8)]
        for k in range(8):
            recips.append(1.0 / a[k][k])
            for j in range(k + 1, 8):
                mult[k][j] = a[k][j] * recips[k]
            for i in range(k + 1, 8):
                for j in range(i, 8):
                    a[i][j] = a[i][j] - mult[k][i] * a[k][j]
            for j in range(k + 1, 8):
                rows[j] = rows[j] - mult[k][j] * rows[k]
        last = STRIPS * (t // STRIPS) + STRIPS
        done = lanes < at + 8
        for k in range(8):
            u = rows[k] * lax.rsqrt(a[k][k])
            w[base // 8 + t, k : k + 1, :] = jnp.where(done, u, 0.0)[0:1]
            if last < 16:
                x[16 + t % STRIPS, k : k + 1, :] = jnp.where(done | (lanes >= 8 * last), u, 0.0)[0:1]
        if t + 1 < last:
            v = [None] * 8
            for i in range(7, -1, -1):
                v[i] = rows[i] * recips[i]
                for j in range(7, i, -1):
                    v[i] = v[i] - mult[i][j] * v[j]
            for s in range(t + 1, last):
                old = x[s]
                new = jnp.where(here, 0.0, old)
                for k in range(8):
                    new = new - lane_of(old, at + k) * v[k]
                x[s] = new
        elif last < 16:
            u = x[16 : 16 + STRIPS].reshape(8 * STRIPS, 128)
            change = dot_t(u, u)[8 * last :].reshape(16 - last, 8, 128)
            inside = (lanes >= 8 * (last - STRIPS)) & (lanes < 8 * last)
            x[last:16] = jnp.where(inside[None], 0.0, x[last:16]) - change


def factor(g, x, w, between):
    def step(k, carry):
        between(k)
        x[0:16] = g[5 * k].reshape(16, 8, 128)
        factor_block(x, w, 128 * k)
        inverse = w[pl.ds(16 * k, 16)].reshape(128, 128)

        def panel(j, c):
            g[4 * k + j] = dot_hi(inverse, g[4 * k + j])
            return c

        lax.fori_loop(k + 1, 4, panel, 0)

        def outer(i, c):
            left = g[4 * k + i]

            def inner(j, cc):
                g[4 * i + j] = g[4 * i + j] - dot_t(left, g[4 * k + j])
                return cc

            return lax.fori_loop(i, 4, inner, c)

        lax.fori_loop(k + 1, 4, outer, 0)
        return carry

    lax.fori_loop(0, 4, step, 0)


TRI = [(i, j) for i in range(4) for j in range(i, 4)]
FAR_FIRST = (4, 3, 5, 2, 6, 1, 7)
NEAR_FIRST = FAR_FIRST[::-1]
MID = 3


def kernel(
    a_hbm, sign_hbm, samp_hbm, o_ref,
    a, sign_ref, samp_ref, om, mate_out, mate_in, own, part_out, part_in, step_out, step_in, full, yt, gloc, gin, gfull, gsq, x, w,
    zf, zs1, zr1, zs2, zr2, zown, pbuf, obuf,
    s_a, s_mate, r_mate, s_part, r_part, s_step, r_step, s_full, r_full, s_fwd, r_fwd,
    s_c, r_c, s_d, r_d, s_e, r_e, s_z1, r_z1, s_z2, r_z2, s_o, r_o,
):
    row, col = lax.axis_index("row"), lax.axis_index("col")
    z, core = col // 2, lax.rem(col, 2)
    py, px = row // 4, lax.rem(row, 4)
    mate = (row, 2 * z + 1 - core)

    def chip(distance):
        return (row, 2 * lax.rem(z + distance, 8) + core)

    def peer(d):
        return lax.rem(row + d, 16)

    def half_rows(which):
        return pl.ds(pl.multiple_of(which * 384, 384), 384)

    small = [
        pltpu.make_async_copy(samp_hbm, samp_ref, s_a.at[2]),
        pltpu.make_async_copy(sign_hbm, sign_ref, s_a.at[3]),
    ]
    for load in small:
        load.start()
    loads = []
    for n, which in enumerate((1 - core, core)):
        loads.append(pltpu.make_async_copy(a_hbm.at[half_rows(which)], a.at[half_rows(which)], s_a.at[n]))
        loads[n].start()
    ready = barrier([mate] + [chip(d) for d in range(1, 8)] + [(peer(d), col) for d in range(1, 16)])

    for load in small:
        load.wait()

    term = lax.broadcasted_iota(jnp.int32, (128, 512), 0)
    for block in range(16):
        parity = lax.population_count(term & samp_ref[block : block + 1, :]) & 1
        om[128 * block : 128 * block + 128, :] = (1 - 2 * parity).astype(F32).astype(BF16)
    signs = (2 * sign_ref[...] - 1).astype(F32).astype(BF16)

    def partial(which, n):
        rows = a[half_rows(which), :] * signs
        return jnp.dot(rows, om[:, 256 * n : 256 * n + 256], preferred_element_type=F32)

    mate_copies, part_copies, step_copies, full_copies, fwd_copies = [], [], [], [], []
    loads[0].wait()
    for n in range(2):
        mate_out[n] = partial(1 - core, n)
        if n == 0:
            ready()
        mate_copies.append(send(mate_out.at[n], mate_in.at[n], s_mate.at[n], r_mate.at[n], mate))
    loads[1].wait()
    for n in range(2):
        own[n] = partial(core, n)
        mate_copies[n].wait_recv()
        own[n] += mate_in[n]
        power = power_of(own[n])
        step_out[n] = jnp.broadcast_to(jnp.exp(power * LN2), (1, 128))
        for d in FAR_FIRST:
            there = lax.rem(z + d, 8)
            part_out[n, d] = coded(own[n, pl.ds(pl.multiple_of(there * 48, 48), 48), :], power)
            part_copies.append(send(part_out.at[n, d], part_in.at[n, d], s_part.at[n, d], r_part.at[n, d], chip(d)))
            step_copies.append(send(step_out.at[n], step_in.at[n, d], s_step.at[n, d], r_step.at[n, d], chip(d)))
    slot = core * 8 + z
    for n in range(2):
        for copy in part_copies[7 * n : 7 * n + 7] + step_copies[7 * n : 7 * n + 7]:
            copy.wait_recv()
        for j in range(2):
            half = slice(128 * j, 128 * j + 128)
            total = own[n, pl.ds(pl.multiple_of(z * 48, 48), 48), half]
            for d in range(1, 8):
                total = total + part_in[n, d, :, half].astype(jnp.int32).astype(F32) * step_in[n, d]
            full[n, slot, :, half] = total.astype(BF16)
        mine = full.at[n, slot]
        for d in FAR_FIRST:
            full_copies.append(send(mine, mine, s_full.at[n, d], r_full.at[n, d], chip(d)))
        fwd_copies.append(send(mine, mine, s_fwd.at[n, 0], r_fwd.at[n, 0], mate))
    for n in range(2):
        for m, d in enumerate(FAR_FIRST):
            full_copies[7 * n + m].wait_recv()
            came = full.at[n, core * 8 + lax.rem(z + 8 - d, 8)]
            fwd_copies.append(send(came, came, s_fwd.at[n, d], r_fwd.at[n, d], mate))
    for copy in fwd_copies:
        copy.wait_recv()

    def piece(r):
        return pl.ds(pl.multiple_of(40 * (2 * r + core), 8), 40)

    for i in range(4):
        yt[128 * i : 128 * i + 128, :] = full[i // 2, :, :, 128 * (i % 2) : 128 * (i % 2) + 128].reshape(768, 128).T
    for i in range(4):
        for n in range(i // 2, 2):
            blocks = jnp.dot(yt[128 * i : 128 * i + 128, :], full[n].reshape(768, 256), preferred_element_type=F32)
            for j in range(2 * n, 2 * n + 2):
                if j >= i:
                    at = 128 * TRI.index((i, j))
                    gloc[at : at + 128, :] = blocks[:, 128 * (j - 2 * n) : 128 * (j - 2 * n) + 128]
    c_copies, d_copies, e_copies, o_copies = [], [], [], []
    for d in range(1, 16):
        c_copies.append(send(gloc.at[piece(peer(d))], gin.at[d], s_c.at[d], r_c.at[d], (peer(d), col)))

    def product(n, carry):
        cols = pl.ds(pl.multiple_of(256 * n, 256), 256)
        zf[:, cols] = jnp.dot(yt[...], a[:, cols], preferred_element_type=F32)
        return carry

    lax.fori_loop(0, 8, product, 0)

    def along(h, d, e):
        return (4 * e + lax.rem(px + d, 4)) if h == 0 else (4 * lax.rem(py + d, 4) + e)

    def first(h, d):
        target = (along(h, d, py if h == 0 else px), col)
        return pltpu.make_async_remote_copy(
            src_ref=zs1.at[h, d], dst_ref=zr1.at[h, d], send_sem=s_z1.at[h, d], recv_sem=r_z1.at[h, d], device_id=target, device_id_type=MESH
        )

    def second(h, d):
        target = (along(1 - h, d, px if h == 0 else py), col)
        return pltpu.make_async_remote_copy(
            src_ref=zs2.at[h, d], dst_ref=zr2.at[h, d], send_sem=s_z2.at[h, d], recv_sem=r_z2.at[h, d], device_id=target, device_id_type=MESH
        )

    def z_part(h, r):
        return zf[256 * h : 256 * h + 256, pl.ds(pl.multiple_of(128 * r, 128), 128)]

    for h in range(2):

        def code(m, carry):
            d, e = m // 4 + 1, lax.rem(m, 4)
            pack(z_part(h, along(h, d, e)), zs1, (h, d, e))
            return carry

        lax.fori_loop(0, 12, code, 0)

    for copy in c_copies:
        copy.wait_recv()
    total = gloc[piece(row), :]
    for d in range(1, 16):
        total = total + gin[d]
    gfull[piece(row), :] = total
    mine = gfull.at[piece(row)]
    for d in range(1, 16):
        d_copies.append(send(mine, mine, s_d.at[d], r_d.at[d], (peer(d), col)))
    e_copies.append(send(mine, mine, s_e.at[0], r_e.at[0], mate))
    for d in range(1, 16):
        d_copies[d - 1].wait_recv()
        came = gfull.at[piece(lax.rem(row + 16 - d, 16))]
        e_copies.append(send(came, came, s_e.at[d], r_e.at[d], mate))
    for d in (2, 1, 3):
        for h in range(2):
            first(h, d).start()
    for copy in e_copies:
        copy.wait_recv()
    for n, (i, j) in enumerate(TRI):
        gsq[4 * i + j] = gfull[128 * n : 128 * n + 128, :]

    def between(k):
        @pl.when(k == MID)
        def _():
            for h in range(2):
                for d in range(1, 4):
                    first(h, d).wait_recv()

                def add(d, carry):
                    e = lax.rem((py if h == 0 else px) + d, 4)
                    value = z_part(h, along(h, 0, e))
                    for f in range(1, 4):
                        step = step_of(zr1[h, f, e, 256:272, :])
                        value = value + zr1[h, f, e, 0:256, :].astype(jnp.int32).astype(F32) * step
                    zown[h, d] = value
                    pack(value, zs2, (h, d))
                    return carry

                lax.fori_loop(0, 4, add, 0)
                for d in range(1, 4):
                    second(h, d).start()

    factor(gsq, x, w, between)

    for h in range(2):
        for d in range(1, 4):
            second(h, d).wait_recv()
        value = zown[h, 0]
        for d in range(1, 4):
            step = step_of(zr2[h, d, 256:272, :])
            value = value + zr2[h, d, 0:256, :].astype(jnp.int32).astype(F32) * step
        pbuf[256 * h : 256 * h + 256, :] = value
    for k in range(4):
        solved = dot_hi(w[16 * k : 16 * k + 16].reshape(128, 128), pbuf[128 * k : 128 * k + 128, :])
        pbuf[128 * k : 128 * k + 128, :] = solved
        for j in range(k + 1, 4):
            pbuf[128 * j : 128 * j + 128, :] -= dot_t(gsq[4 * k + j], solved)

    for d in range(1, 16):
        part = pl.ds(pl.multiple_of(32 * peer(d), 32), 32)
        o_copies.append(send(pbuf.at[part], obuf.at[row], s_o.at[d], r_o.at[d], (peer(d), col)))
    obuf[row] = pbuf[pl.ds(pl.multiple_of(32 * row, 32), 32), :]
    for copy in o_copies:
        copy.wait_recv()
    for r in range(16):
        o_ref[:, 128 * r : 128 * r + 128] = obuf[r]
    for copy in mate_copies + part_copies + step_copies + full_copies + fwd_copies + c_copies + d_copies + e_copies + o_copies:
        copy.wait_send()
    for h in range(2):
        for d in range(1, 4):
            first(h, d).wait_send()
            second(h, d).wait_send()


def shards(term_matrix, sign_bits, sampled):
    vmem = pl.BlockSpec(memory_space=pltpu.VMEM)
    dma = pltpu.SemaphoreType.DMA
    return pl.pallas_call(
        kernel,
        out_shape=jax.ShapeDtypeStruct((32, 2048), F32),
        in_specs=[pl.BlockSpec(memory_space=pl.ANY)] * 3,
        out_specs=vmem,
        scratch_shapes=[
            pltpu.VMEM((768, 2048), BF16),
            pltpu.VMEM((1, 2048), jnp.int32),
            pltpu.VMEM((16, 512), jnp.int32),
            pltpu.VMEM((2048, 512), BF16),
            pltpu.VMEM((2, 384, 256), F32),
            pltpu.VMEM((2, 384, 256), F32),
            pltpu.VMEM((2, 384, 256), F32),
            pltpu.VMEM((2, 8, 48, 256), jnp.int16),
            pltpu.VMEM((2, 8, 48, 256), jnp.int16),
            pltpu.VMEM((2, 1, 128), F32),
            pltpu.VMEM((2, 8, 1, 128), F32),
            pltpu.VMEM((2, 16, 48, 256), BF16),
            pltpu.VMEM((512, 768), BF16),
            pltpu.VMEM((1280, 128), F32),
            pltpu.VMEM((16, 40, 128), F32),
            pltpu.VMEM((1280, 128), F32),
            pltpu.VMEM((16, 128, 128), F32),
            pltpu.VMEM((32, 8, 128), F32),
            pltpu.VMEM((64, 8, 128), F32),
            pltpu.VMEM((512, 2048), F32),
            pltpu.VMEM((2, 4, 4, 272, 128), jnp.int16),
            pltpu.VMEM((2, 4, 4, 272, 128), jnp.int16),
            pltpu.VMEM((2, 4, 272, 128), jnp.int16),
            pltpu.VMEM((2, 4, 272, 128), jnp.int16),
            pltpu.VMEM((2, 4, 256, 128), F32),
            pltpu.VMEM((512, 128), F32),
            pltpu.VMEM((16, 32, 128), F32),
            dma((4,)),
        ]
        + [dma((2,))] * 2
        + [dma((2, 8))] * 8
        + [dma((16,))] * 6
        + [dma((2, 4))] * 4
        + [dma((16,))] * 2,
        compiler_params=pltpu.CompilerParams(collective_id=0, has_side_effects=True, vmem_limit_bytes=60 << 20),
    )(term_matrix, sign_bits.reshape(1, 2048), sampled)


def solution(mesh):
    in_specs = (P("row", "col"), P("col"), P("col", None))
    return jax.shard_map(shards, mesh=mesh, in_specs=in_specs, out_specs=P("row", "col"), check_vma=False)
```

```python
import jax
import jax.numpy as jnp
from jax import lax
from jax.experimental import pallas as pl
from jax.experimental.pallas import tpu as pltpu
from jax.sharding import PartitionSpec as P

MESH = pl.DeviceIdType.MESH
F32 = jnp.float32
BF16 = jnp.bfloat16
STRIPS = 4
LN2 = 0.6931471805599453


def barrier(targets):
    sem = pltpu.get_barrier_semaphore()
    for target in targets:
        pl.semaphore_signal(sem, inc=1, device_id=target, device_id_type=MESH)
    return lambda: pl.semaphore_wait(sem, len(targets))


def send(src, dst, send_sem, recv_sem, target):
    copy = pltpu.make_async_remote_copy(
        src_ref=src, dst_ref=dst, send_sem=send_sem, recv_sem=recv_sem, device_id=target, device_id_type=MESH
    )
    copy.start()
    return copy


def power_of(value):
    top = jnp.max(jnp.max(jnp.abs(value), axis=0, keepdims=True), axis=1, keepdims=True)
    return jnp.ceil(jnp.log(jnp.maximum(top, 1e-30)) * (1.0 / LN2)) - 14.0


def coded(value, power):
    return jnp.floor(value * jnp.exp(power * -LN2) + 0.5).astype(jnp.int32).astype(jnp.int16)


def pack(value, ref, at):
    power = power_of(value)
    ref[at + (slice(0, 256),)] = coded(value, power)
    ref[at + (slice(256, 272),)] = jnp.broadcast_to(power, (16, 128)).astype(jnp.int32).astype(jnp.int16)


def step_of(power):
    return jnp.exp(power.astype(jnp.int32).astype(F32) * LN2)[0:1, :]


AHEAD = 2


def lane_of(x, lane):
    return jnp.broadcast_to(x[:, lane : lane + 1], (8, 128))


def split(u):
    high = u.astype(BF16)
    rest = u - high.astype(F32)
    mid = rest.astype(BF16)
    return high, mid, (rest - mid.astype(F32)).astype(BF16)


def dot_t(a, b):
    ah, am, al = split(a)
    bh, bm, bl = split(b)
    left = jnp.concatenate([ah, ah, am, ah, am, al], 0)
    right = jnp.concatenate([bh, bm, bh, bl, bm, bh], 0)
    return lax.dot_general(left, right, (((0,), (0,)), ((), ())), preferred_element_type=F32)


def dot_hi(a, b):
    ah, am, al = split(a)
    bh, bm, bl = split(b)
    left = jnp.concatenate([ah, ah, am, ah, am, al], 1)
    right = jnp.concatenate([bh, bm, bh, bl, bm, bh], 0)
    return jnp.dot(left, right, preferred_element_type=F32)


def dot_mid(a, b, axis):
    ah, am, _ = split(a)
    bh, bm, _ = split(b)
    left = jnp.concatenate([ah, ah, am], axis)
    right = jnp.concatenate([bh, bm, bh], 0)
    return lax.dot_general(left, right, (((axis,), (0,)), ((), ())), preferred_element_type=F32)


def factor_block(x, w, base):
    lanes = lax.broadcasted_iota(jnp.int32, (8, 128), 1)
    for t in range(16):
        at = 8 * t
        strip = x[t]
        for j in range(8):
            x[24 + j] = lane_of(strip, at + j)
        here = (lanes >= at) & (lanes < at + 8)
        a = [[None] * 8 for _ in range(8)]
        for i in range(8):
            for j in range(i, 8):
                a[i][j] = jnp.broadcast_to(x[24 + j, i : i + 1, :], (8, 128))
        rows = [jnp.where(here, (lanes == at + i).astype(F32), jnp.broadcast_to(x[t, i : i + 1, :], (8, 128))) for i in range(8)]
        recips, mult = [], [[None] * 8 for _ in range(8)]
        for k in range(8):
            recips.append(1.0 / a[k][k])
            for j in range(k + 1, 8):
                mult[k][j] = a[k][j] * recips[k]
            for i in range(k + 1, 8):
                for j in range(i, 8):
                    a[i][j] = a[i][j] - mult[k][i] * a[k][j]
            for j in range(k + 1, 8):
                rows[j] = rows[j] - mult[k][j] * rows[k]
        last = STRIPS * (t // STRIPS) + STRIPS
        reach = min(last + AHEAD, 16)
        done = lanes < at + 8
        for k in range(8):
            u = rows[k] * lax.rsqrt(a[k][k])
            w[base // 8 + t, k : k + 1, :] = jnp.where(done, u, 0.0)[0:1]
            if reach < 16:
                x[16 + t % STRIPS, k : k + 1, :] = jnp.where(done | (lanes >= 8 * last), u, 0.0)[0:1]
        scaled = [rows[k] * recips[k] for k in range(8)]
        for s in range(t + 1, reach):
            old = x[s]
            new = jnp.where(here, 0.0, old)
            c = [lane_of(old, at + k) for k in range(8)]
            for k in range(8):
                for j in range(k):
                    c[k] = c[k] - c[j] * mult[j][k]
                new = new - c[k] * scaled[k]
            x[s] = new
        if t + 1 == last and reach < 16:
            u = x[16 : 16 + STRIPS].reshape(8 * STRIPS, 128)
            change = dot_t(u, u)[8 * reach :].reshape(16 - reach, 8, 128)
            inside = (lanes >= 8 * (last - STRIPS)) & (lanes < 8 * last)
            x[reach:16] = jnp.where(inside[None], 0.0, x[reach:16]) - change


def factor(g, x, w, between):
    def step(k, carry):
        between(k)
        x[0:16] = g[k, :, pl.ds(pl.multiple_of(128 * k, 128), 128)].reshape(16, 8, 128)
        factor_block(x, w, 128 * k)

        @pl.when(k < 3)
        def _():
            panel = dot_hi(w[pl.ds(16 * k, 16)].reshape(128, 128), g[k])
            g[k] = panel
            change = dot_t(panel, panel)
            for i in range(1, 4):

                @pl.when(i > k)
                def _():
                    g[i] = g[i] - change[128 * i : 128 * i + 128]

        return carry

    lax.fori_loop(0, 4, step, 0)


TRI = [(i, j) for i in range(4) for j in range(i, 4)]
FAR_FIRST = (4, 3, 5, 2, 6, 1, 7)
NEAR_FIRST = FAR_FIRST[::-1]
MID = 3


def kernel(
    a_hbm, sign_hbm, samp_hbm, o_ref,
    a, sign_ref, samp_ref, om, mate_out, mate_in, own, part_out, part_in, step_out, step_in, full, yt, gloc, gin, gfull, gsq, x, w,
    zf, zs1, zr1, zt1, zu1, zs2, zr2, zown, pbuf, obuf,
    s_a, s_mate, r_mate, s_part, r_part, s_step, r_step, s_full, r_full, s_fwd, r_fwd,
    s_c, r_c, s_d, r_d, s_e, r_e, s_z1, r_z1, s_t1, r_t1, s_z2, r_z2, s_o, r_o,
):
    row, col = lax.axis_index("row"), lax.axis_index("col")
    z, core = col // 2, lax.rem(col, 2)
    py, px = row // 4, lax.rem(row, 4)
    mate = (row, 2 * z + 1 - core)

    def chip(distance):
        return (row, 2 * lax.rem(z + distance, 8) + core)

    def peer(d):
        return lax.rem(row + d, 16)

    def half_rows(which):
        return pl.ds(pl.multiple_of(which * 384, 384), 384)

    small = [
        pltpu.make_async_copy(samp_hbm, samp_ref, s_a.at[2]),
        pltpu.make_async_copy(sign_hbm, sign_ref, s_a.at[3]),
    ]
    for load in small:
        load.start()
    loads = []
    for n, which in enumerate((1 - core, core)):
        loads.append(pltpu.make_async_copy(a_hbm.at[half_rows(which)], a.at[half_rows(which)], s_a.at[n]))
        loads[n].start()
    ready = barrier([mate] + [chip(d) for d in range(1, 8)] + [(peer(d), col) for d in range(1, 16)])

    for load in small:
        load.wait()

    term = lax.broadcasted_iota(jnp.int32, (128, 512), 0)
    for block in range(16):
        parity = lax.population_count(term & samp_ref[block : block + 1, :]) & 1
        om[128 * block : 128 * block + 128, :] = (1 - 2 * parity).astype(F32).astype(BF16)
    signs = (2 * sign_ref[...] - 1).astype(F32).astype(BF16)

    def partial(which, n):
        rows = a[half_rows(which), :] * signs
        return jnp.dot(rows, om[:, 256 * n : 256 * n + 256], preferred_element_type=F32)

    mate_copies, part_copies, step_copies, full_copies, fwd_copies = [], [], [], [], []
    loads[0].wait()
    for n in range(2):
        mate_out[n] = partial(1 - core, n)
        if n == 0:
            ready()
        mate_copies.append(send(mate_out.at[n], mate_in.at[n], s_mate.at[n], r_mate.at[n], mate))
    loads[1].wait()
    for n in range(2):
        own[n] = partial(core, n)
        mate_copies[n].wait_recv()
        own[n] += mate_in[n]
        power = power_of(own[n])
        step_out[n] = jnp.broadcast_to(jnp.exp(power * LN2), (1, 128))
        for d in FAR_FIRST:
            there = lax.rem(z + d, 8)
            part_out[n, d] = coded(own[n, pl.ds(pl.multiple_of(there * 48, 48), 48), :], power)
            part_copies.append(send(part_out.at[n, d], part_in.at[n, d], s_part.at[n, d], r_part.at[n, d], chip(d)))
            step_copies.append(send(step_out.at[n], step_in.at[n, d], s_step.at[n, d], r_step.at[n, d], chip(d)))
    slot = core * 8 + z
    for n in range(2):
        for copy in part_copies[7 * n : 7 * n + 7] + step_copies[7 * n : 7 * n + 7]:
            copy.wait_recv()
        for j in range(2):
            half = slice(128 * j, 128 * j + 128)
            total = own[n, pl.ds(pl.multiple_of(z * 48, 48), 48), half]
            for d in range(1, 8):
                total = total + part_in[n, d, :, half].astype(jnp.int32).astype(F32) * step_in[n, d]
            full[n, slot, :, half] = total.astype(BF16)
        mine = full.at[n, slot]
        for d in FAR_FIRST:
            full_copies.append(send(mine, mine, s_full.at[n, d], r_full.at[n, d], chip(d)))
        fwd_copies.append(send(mine, mine, s_fwd.at[n, 0], r_fwd.at[n, 0], mate))
    def piece(r):
        return pl.ds(pl.multiple_of(40 * (2 * r + core), 8), 40)

    def gram(i, n):
        blocks = jnp.dot(yt[128 * i : 128 * i + 128, :], full[n].reshape(768, 256), preferred_element_type=F32)
        for j in range(2 * n, 2 * n + 2):
            if j >= i:
                at = 128 * TRI.index((i, j))
                gloc[at : at + 128, :] = blocks[:, 128 * (j - 2 * n) : 128 * (j - 2 * n) + 128]

    def product(h):
        def columns(m, carry):
            cols = pl.ds(pl.multiple_of(256 * m, 256), 256)
            zf[256 * h : 256 * h + 256, cols] = jnp.dot(yt[256 * h : 256 * h + 256, :], a[:, cols], preferred_element_type=F32)
            return carry

        lax.fori_loop(0, 8, columns, 0)

    c_copies, d_copies, e_copies = [], [], []
    for n in range(2):
        for m, d in enumerate(FAR_FIRST):
            full_copies[7 * n + m].wait_recv()
            came = full.at[n, core * 8 + lax.rem(z + 8 - d, 8)]
            fwd_copies.append(send(came, came, s_fwd.at[n, d], r_fwd.at[n, d], mate))
        for copy in fwd_copies[n : n + 1] + fwd_copies[2 + 7 * n : 9 + 7 * n]:
            copy.wait_recv()
        for i in range(2 * n, 2 * n + 2):
            yt[128 * i : 128 * i + 128, :] = full[n, :, :, 128 * (i % 2) : 128 * (i % 2) + 128].reshape(768, 128).T
        for i in range(2 * n + 2):
            gram(i, n)
        if n == 0:
            product(0)
    for d in range(1, 16):
        c_copies.append(send(gloc.at[piece(peer(d))], gin.at[d], s_c.at[d], r_c.at[d], (peer(d), col)))
    product(1)

    def along(h, d, e):
        return (4 * e + lax.rem(px + d, 4)) if h == 0 else (4 * lax.rem(py + d, 4) + e)

    def first(h, d):
        target = (along(h, d, py if h == 0 else px), col)
        return pltpu.make_async_remote_copy(
            src_ref=zs1.at[h, d], dst_ref=zr1.at[h, d], send_sem=s_z1.at[h, d], recv_sem=r_z1.at[h, d], device_id=target, device_id_type=MESH
        )

    def first_steps(h, d):
        target = (along(h, d, py if h == 0 else px), col)
        return pltpu.make_async_remote_copy(
            src_ref=zt1.at[h, d], dst_ref=zu1.at[h, d], send_sem=s_t1.at[h, d], recv_sem=r_t1.at[h, d], device_id=target, device_id_type=MESH
        )

    def second(h, d):
        target = (along(1 - h, d, px if h == 0 else py), col)
        return pltpu.make_async_remote_copy(
            src_ref=zs2.at[h, d], dst_ref=zr2.at[h, d], send_sem=s_z2.at[h, d], recv_sem=r_z2.at[h, d], device_id=target, device_id_type=MESH
        )

    def z_part(h, r):
        return zf[256 * h : 256 * h + 256, pl.ds(pl.multiple_of(128 * r, 128), 128)]

    for h in range(2):

        def code(m, carry):
            d, e = m // 4 + 1, lax.rem(m, 4)
            value = z_part(h, along(h, d, e))
            power = power_of(value)
            zs1[h, d, e] = coded(value, power)
            zt1[h, d, e] = jnp.broadcast_to(jnp.exp(power * LN2), (1, 128))
            return carry

        lax.fori_loop(0, 12, code, 0)

    for copy in c_copies:
        copy.wait_recv()
    total = gloc[piece(row), :]
    for d in range(1, 16):
        total = total + gin[d]
    gfull[piece(row), :] = total
    mine = gfull.at[piece(row)]
    for d in range(1, 16):
        d_copies.append(send(mine, mine, s_d.at[d], r_d.at[d], (peer(d), col)))
    e_copies.append(send(mine, mine, s_e.at[0], r_e.at[0], mate))
    for d in range(1, 16):
        d_copies[d - 1].wait_recv()
        came = gfull.at[piece(lax.rem(row + 16 - d, 16))]
        e_copies.append(send(came, came, s_e.at[d], r_e.at[d], mate))
    for d in (2, 1, 3):
        for h in range(2):
            first_steps(h, d).start()
            first(h, d).start()
    for copy in e_copies:
        copy.wait_recv()
    for i in range(1, 4):
        gsq[i, :, 0 : 128 * i] = jnp.zeros((128, 128 * i), F32)
    for n, (i, j) in enumerate(TRI):
        gsq[i, :, 128 * j : 128 * j + 128] = gfull[128 * n : 128 * n + 128, :]

    def between(k):
        @pl.when(k == MID)
        def _():
            for h in range(2):
                for d in range(1, 4):
                    first(h, d).wait_recv()
                    first_steps(h, d).wait_recv()

                def add(d, carry):
                    e = lax.rem((py if h == 0 else px) + d, 4)
                    value = z_part(h, along(h, 0, e))
                    for f in range(1, 4):
                        value = value + zr1[h, f, e].astype(jnp.int32).astype(F32) * zu1[h, f, e]
                    zown[h, d] = value
                    pack(value, zs2, (h, d))
                    return carry

                lax.fori_loop(0, 4, add, 0)
                for d in range(1, 4):
                    second(h, d).start()

    factor(gsq, x, w, between)

    def out_copy(there, here):
        return pltpu.make_async_remote_copy(
            src_ref=pbuf.at[pl.ds(pl.multiple_of(32 * there, 32), 32)], dst_ref=obuf.at[here],
            send_sem=s_o.at[there], recv_sem=r_o.at[here], device_id=(there, col), device_id_type=MESH,
        )

    for k in range(4):
        h = k // 2
        if k % 2 == 0:
            for d in range(1, 4):
                second(h, d).wait_recv()
            value = zown[h, 0]
            for d in range(1, 4):
                step = step_of(zr2[h, d, 256:272, :])
                value = value + zr2[h, d, 0:256, :].astype(jnp.int32).astype(F32) * step
            if h == 1:
                for j in range(2):
                    value = value - dot_mid(gsq[j, :, 256:512], pbuf[128 * j : 128 * j + 128, :], 0)
            pbuf[256 * h : 256 * h + 256, :] = value
        solved = dot_mid(w[16 * k : 16 * k + 16].reshape(128, 128), pbuf[128 * k : 128 * k + 128, :], 1)
        pbuf[128 * k : 128 * k + 128, :] = solved
        for there in range(4 * k, 4 * k + 4):

            @pl.when(row != there)
            def _():
                out_copy(there, row).start()

        if k % 2 == 0:
            after = slice(128 * k + 128, 128 * k + 256)
            pbuf[after, :] -= dot_mid(gsq[k, :, after], solved, 0)

    obuf[row] = pbuf[pl.ds(pl.multiple_of(32 * row, 32), 32), :]
    for d in range(1, 16):
        out_copy(row, peer(d)).wait_recv()
    for r in range(16):
        o_ref[:, 128 * r : 128 * r + 128] = obuf[r]
    for copy in mate_copies + part_copies + step_copies + full_copies + fwd_copies + c_copies + d_copies + e_copies:
        copy.wait_send()
    for there in range(16):

        @pl.when(row != there)
        def _():
            out_copy(there, row).wait_send()

    for h in range(2):
        for d in range(1, 4):
            first(h, d).wait_send()
            first_steps(h, d).wait_send()
            second(h, d).wait_send()


def shards(term_matrix, sign_bits, sampled):
    vmem = pl.BlockSpec(memory_space=pltpu.VMEM)
    dma = pltpu.SemaphoreType.DMA
    return pl.pallas_call(
        kernel,
        out_shape=jax.ShapeDtypeStruct((32, 2048), F32),
        in_specs=[pl.BlockSpec(memory_space=pl.ANY)] * 3,
        out_specs=vmem,
        scratch_shapes=[
            pltpu.VMEM((768, 2048), BF16),
            pltpu.VMEM((1, 2048), jnp.int32),
            pltpu.VMEM((16, 512), jnp.int32),
            pltpu.VMEM((2048, 512), BF16),
            pltpu.VMEM((2, 384, 256), F32),
            pltpu.VMEM((2, 384, 256), F32),
            pltpu.VMEM((2, 384, 256), F32),
            pltpu.VMEM((2, 8, 48, 256), jnp.int16),
            pltpu.VMEM((2, 8, 48, 256), jnp.int16),
            pltpu.VMEM((2, 1, 128), F32),
            pltpu.VMEM((2, 8, 1, 128), F32),
            pltpu.VMEM((2, 16, 48, 256), BF16),
            pltpu.VMEM((512, 768), BF16),
            pltpu.VMEM((1280, 128), F32),
            pltpu.VMEM((16, 40, 128), F32),
            pltpu.VMEM((1280, 128), F32),
            pltpu.VMEM((4, 128, 512), F32),
            pltpu.VMEM((32, 8, 128), F32),
            pltpu.VMEM((64, 8, 128), F32),
            pltpu.VMEM((512, 2048), F32),
            pltpu.VMEM((2, 4, 4, 256, 128), jnp.int16),
            pltpu.VMEM((2, 4, 4, 256, 128), jnp.int16),
            pltpu.VMEM((2, 4, 4, 1, 128), F32),
            pltpu.VMEM((2, 4, 4, 1, 128), F32),
            pltpu.VMEM((2, 4, 272, 128), jnp.int16),
            pltpu.VMEM((2, 4, 272, 128), jnp.int16),
            pltpu.VMEM((2, 4, 256, 128), F32),
            pltpu.VMEM((512, 128), F32),
            pltpu.VMEM((16, 32, 128), F32),
            dma((4,)),
        ]
        + [dma((2,))] * 2
        + [dma((2, 8))] * 8
        + [dma((16,))] * 6
        + [dma((2, 4))] * 6
        + [dma((16,))] * 2,
        compiler_params=pltpu.CompilerParams(collective_id=0, has_side_effects=True, vmem_limit_bytes=60 << 20),
    )(term_matrix, sign_bits.reshape(1, 2048), sampled)


def solution(mesh):
    in_specs = (P("row", "col"), P("col"), P("col", None))
    return jax.shard_map(shards, mesh=mesh, in_specs=in_specs, out_specs=P("row", "col"), check_vma=False)
```

```python
import jax
import jax.numpy as jnp
from jax import lax
from jax.experimental import pallas as pl
from jax.experimental.pallas import tpu as pltpu
from jax.sharding import PartitionSpec as P

MESH = pl.DeviceIdType.MESH
F32 = jnp.float32
BF16 = jnp.bfloat16
STRIPS = 4
LN2 = 0.6931471805599453


def barrier(targets):
    sem = pltpu.get_barrier_semaphore()
    for target in targets:
        pl.semaphore_signal(sem, inc=1, device_id=target, device_id_type=MESH)
    return lambda: pl.semaphore_wait(sem, len(targets))


def send(src, dst, send_sem, recv_sem, target):
    copy = pltpu.make_async_remote_copy(
        src_ref=src, dst_ref=dst, send_sem=send_sem, recv_sem=recv_sem, device_id=target, device_id_type=MESH
    )
    copy.start()
    return copy


def power_of(value):
    top = jnp.max(jnp.max(jnp.abs(value), axis=0, keepdims=True), axis=1, keepdims=True)
    return jnp.ceil(jnp.log(jnp.maximum(top, 1e-30)) * (1.0 / LN2)) - 14.0


def coded(value, power):
    return jnp.floor(value * jnp.exp(power * -LN2) + 0.5).astype(jnp.int32).astype(jnp.int16)


def pack(value, ref, at):
    power = power_of(value)
    ref[at + (slice(0, 256),)] = coded(value, power)
    ref[at + (slice(256, 272),)] = jnp.broadcast_to(power, (16, 128)).astype(jnp.int32).astype(jnp.int16)


def step_of(power):
    return jnp.exp(power.astype(jnp.int32).astype(F32) * LN2)[0:1, :]


AHEAD = 2


def lane_of(x, lane):
    return jnp.broadcast_to(x[:, lane : lane + 1], (8, 128))


def split(u):
    high = u.astype(BF16)
    return high, (u - high.astype(F32)).astype(BF16)


def dot_t(a, b):
    ah, am = split(a)
    bh, bm = split(b)
    left = jnp.concatenate([ah, ah, am], 0)
    right = jnp.concatenate([bh, bm, bh], 0)
    return lax.dot_general(left, right, (((0,), (0,)), ((), ())), preferred_element_type=F32)


def dot_hi(a, b):
    ah, am = split(a)
    bh, bm = split(b)
    left = jnp.concatenate([ah, ah, am], 1)
    right = jnp.concatenate([bh, bm, bh], 0)
    return jnp.dot(left, right, preferred_element_type=F32)


def factor_block(x, w, base):
    lanes = lax.broadcasted_iota(jnp.int32, (8, 128), 1)
    for t in range(16):
        at = 8 * t
        strip = x[t]
        for j in range(8):
            x[24 + j] = lane_of(strip, at + j)
        here = (lanes >= at) & (lanes < at + 8)
        a = [[None] * 8 for _ in range(8)]
        for i in range(8):
            for j in range(i, 8):
                a[i][j] = jnp.broadcast_to(x[24 + j, i : i + 1, :], (8, 128))
        rows = [jnp.where(here, (lanes == at + i).astype(F32), jnp.broadcast_to(x[t, i : i + 1, :], (8, 128))) for i in range(8)]
        recips, mult = [], [[None] * 8 for _ in range(8)]
        for k in range(8):
            recips.append(1.0 / a[k][k])
            for j in range(k + 1, 8):
                mult[k][j] = a[k][j] * recips[k]
            for i in range(k + 1, 8):
                for j in range(i, 8):
                    a[i][j] = a[i][j] - mult[k][i] * a[k][j]
            for j in range(k + 1, 8):
                rows[j] = rows[j] - mult[k][j] * rows[k]
        last = STRIPS * (t // STRIPS) + STRIPS
        reach = min(last + AHEAD, 16)
        done = lanes < at + 8
        for k in range(8):
            u = rows[k] * lax.rsqrt(a[k][k])
            w[base // 8 + t, k : k + 1, :] = jnp.where(done, u, 0.0)[0:1]
            if reach < 16:
                x[16 + t % STRIPS, k : k + 1, :] = jnp.where(done | (lanes >= 8 * last), u, 0.0)[0:1]
        scaled = [rows[k] * recips[k] for k in range(8)]
        for s in range(t + 1, reach):
            old = x[s]
            new = jnp.where(here, 0.0, old)
            c = [lane_of(old, at + k) for k in range(8)]
            for k in range(8):
                for j in range(k):
                    c[k] = c[k] - c[j] * mult[j][k]
                new = new - c[k] * scaled[k]
            x[s] = new
        if t + 1 == last and reach < 16:
            u = x[16 : 16 + STRIPS].reshape(8 * STRIPS, 128)
            change = dot_t(u, u)[8 * reach :].reshape(16 - reach, 8, 128)
            inside = (lanes >= 8 * (last - STRIPS)) & (lanes < 8 * last)
            x[reach:16] = jnp.where(inside[None], 0.0, x[reach:16]) - change


def factor(g, x, w, between):
    def step(k, carry):
        between(k)
        x[0:16] = g[k, :, pl.ds(pl.multiple_of(128 * k, 128), 128)].reshape(16, 8, 128)
        factor_block(x, w, 128 * k)

        @pl.when(k < 3)
        def _():
            panel = dot_hi(w[pl.ds(16 * k, 16)].reshape(128, 128), g[k])
            g[k] = panel
            change = dot_t(panel, panel)
            for i in range(1, 4):

                @pl.when(i > k)
                def _():
                    g[i] = g[i] - change[128 * i : 128 * i + 128]

        return carry

    lax.fori_loop(0, 4, step, 0)


TRI = [(i, j) for i in range(4) for j in range(i, 4)]
FAR_FIRST = (4, 3, 5, 2, 6, 1, 7)
NEAR_FIRST = FAR_FIRST[::-1]
MID = 3


def kernel(
    a_hbm, sign_hbm, samp_hbm, o_ref,
    a, sign_ref, samp_ref, om, mate_out, mate_in, own, part_out, part_in, step_out, step_in, full, yt, gloc, gin, gfull, gsq, x, w,
    zf, zs1, zr1, zt1, zu1, zs2, zr2, zown, pbuf, obuf,
    s_a, s_mate, r_mate, s_part, r_part, s_step, r_step, s_full, r_full, s_fwd, r_fwd,
    s_c, r_c, s_d, r_d, s_e, r_e, s_z1, r_z1, s_t1, r_t1, s_z2, r_z2, s_o, r_o,
):
    row, col = lax.axis_index("row"), lax.axis_index("col")
    z, core = col // 2, lax.rem(col, 2)
    py, px = row // 4, lax.rem(row, 4)
    mate = (row, 2 * z + 1 - core)

    def chip(distance):
        return (row, 2 * lax.rem(z + distance, 8) + core)

    def peer(d):
        return lax.rem(row + d, 16)

    def half_rows(which):
        return pl.ds(pl.multiple_of(which * 384, 384), 384)

    small = [
        pltpu.make_async_copy(samp_hbm, samp_ref, s_a.at[2]),
        pltpu.make_async_copy(sign_hbm, sign_ref, s_a.at[3]),
    ]
    for load in small:
        load.start()
    loads = []
    for n, which in enumerate((1 - core, core)):
        loads.append(pltpu.make_async_copy(a_hbm.at[half_rows(which)], a.at[half_rows(which)], s_a.at[n]))
        loads[n].start()
    ready = barrier([mate] + [chip(d) for d in range(1, 8)] + [(peer(d), col) for d in range(1, 16)])

    for load in small:
        load.wait()

    term = lax.broadcasted_iota(jnp.int32, (128, 512), 0)
    for block in range(16):
        parity = lax.population_count(term & samp_ref[block : block + 1, :]) & 1
        om[128 * block : 128 * block + 128, :] = (1 - 2 * parity).astype(F32).astype(BF16)
    signs = (2 * sign_ref[...] - 1).astype(F32).astype(BF16)

    def partial(which, n):
        rows = a[half_rows(which), :] * signs
        return jnp.dot(rows, om[:, 256 * n : 256 * n + 256], preferred_element_type=F32)

    mate_copies, part_copies, step_copies, full_copies, fwd_copies = [], [], [], [], []
    loads[0].wait()
    for n in range(2):
        mate_out[n] = partial(1 - core, n)
        if n == 0:
            ready()
        mate_copies.append(send(mate_out.at[n], mate_in.at[n], s_mate.at[n], r_mate.at[n], mate))
    loads[1].wait()
    for n in range(2):
        own[n] = partial(core, n)
        mate_copies[n].wait_recv()
        own[n] += mate_in[n]
        power = power_of(own[n])
        step_out[n] = jnp.broadcast_to(jnp.exp(power * LN2), (1, 128))
        for d in FAR_FIRST:
            there = lax.rem(z + d, 8)
            part_out[n, d] = coded(own[n, pl.ds(pl.multiple_of(there * 48, 48), 48), :], power)
            part_copies.append(send(part_out.at[n, d], part_in.at[n, d], s_part.at[n, d], r_part.at[n, d], chip(d)))
            step_copies.append(send(step_out.at[n], step_in.at[n, d], s_step.at[n, d], r_step.at[n, d], chip(d)))
    slot = core * 8 + z
    for n in range(2):
        for copy in part_copies[7 * n : 7 * n + 7] + step_copies[7 * n : 7 * n + 7]:
            copy.wait_recv()
        for j in range(2):
            half = slice(128 * j, 128 * j + 128)
            total = own[n, pl.ds(pl.multiple_of(z * 48, 48), 48), half]
            for d in range(1, 8):
                total = total + part_in[n, d, :, half].astype(jnp.int32).astype(F32) * step_in[n, d]
            full[n, slot, :, half] = total.astype(BF16)
        mine = full.at[n, slot]
        for d in FAR_FIRST:
            full_copies.append(send(mine, mine, s_full.at[n, d], r_full.at[n, d], chip(d)))
        fwd_copies.append(send(mine, mine, s_fwd.at[n, 0], r_fwd.at[n, 0], mate))
    def piece(r):
        return pl.ds(pl.multiple_of(40 * (2 * r + core), 8), 40)

    def gram(i, n):
        blocks = jnp.dot(yt[128 * i : 128 * i + 128, :], full[n].reshape(768, 256), preferred_element_type=F32)
        for j in range(2 * n, 2 * n + 2):
            if j >= i:
                at = 128 * TRI.index((i, j))
                gloc[at : at + 128, :] = blocks[:, 128 * (j - 2 * n) : 128 * (j - 2 * n) + 128]

    def product(h):
        def columns(m, carry):
            cols = pl.ds(pl.multiple_of(256 * m, 256), 256)
            zf[256 * h : 256 * h + 256, cols] = jnp.dot(yt[256 * h : 256 * h + 256, :], a[:, cols], preferred_element_type=F32)
            return carry

        lax.fori_loop(0, 8, columns, 0)

    c_copies, d_copies, e_copies = [], [], []
    for n in range(2):
        for m, d in enumerate(FAR_FIRST):
            full_copies[7 * n + m].wait_recv()
            came = full.at[n, core * 8 + lax.rem(z + 8 - d, 8)]
            fwd_copies.append(send(came, came, s_fwd.at[n, d], r_fwd.at[n, d], mate))
        if n == 1:
            product(0)
        for copy in fwd_copies[n : n + 1] + fwd_copies[2 + 7 * n : 9 + 7 * n]:
            copy.wait_recv()
        for i in range(2 * n, 2 * n + 2):
            yt[128 * i : 128 * i + 128, :] = full[n, :, :, 128 * (i % 2) : 128 * (i % 2) + 128].reshape(768, 128).T
        for i in range(2 * n + 2):
            gram(i, n)
    for d in range(1, 16):
        c_copies.append(send(gloc.at[piece(peer(d))], gin.at[d], s_c.at[d], r_c.at[d], (peer(d), col)))
    product(1)

    def along(h, d, e):
        return (4 * e + lax.rem(px + d, 4)) if h == 0 else (4 * lax.rem(py + d, 4) + e)

    def first(h, d):
        target = (along(h, d, py if h == 0 else px), col)
        return pltpu.make_async_remote_copy(
            src_ref=zs1.at[h, d], dst_ref=zr1.at[h, d], send_sem=s_z1.at[h, d], recv_sem=r_z1.at[h, d], device_id=target, device_id_type=MESH
        )

    def first_steps(h, d):
        target = (along(h, d, py if h == 0 else px), col)
        return pltpu.make_async_remote_copy(
            src_ref=zt1.at[h, d], dst_ref=zu1.at[h, d], send_sem=s_t1.at[h, d], recv_sem=r_t1.at[h, d], device_id=target, device_id_type=MESH
        )

    def second(h, d):
        target = (along(1 - h, d, px if h == 0 else py), col)
        return pltpu.make_async_remote_copy(
            src_ref=zs2.at[h, d], dst_ref=zr2.at[h, d], send_sem=s_z2.at[h, d], recv_sem=r_z2.at[h, d], device_id=target, device_id_type=MESH
        )

    def z_part(h, r):
        return zf[256 * h : 256 * h + 256, pl.ds(pl.multiple_of(128 * r, 128), 128)]

    for h in range(2):

        def code(m, carry):
            d, e = m // 4 + 1, lax.rem(m, 4)
            value = z_part(h, along(h, d, e))
            power = power_of(value)
            zs1[h, d, e] = coded(value, power)
            zt1[h, d, e] = jnp.broadcast_to(jnp.exp(power * LN2), (1, 128))
            return carry

        lax.fori_loop(0, 12, code, 0)

    for copy in c_copies:
        copy.wait_recv()
    total = gloc[piece(row), :]
    for d in range(1, 16):
        total = total + gin[d]
    gfull[piece(row), :] = total
    mine = gfull.at[piece(row)]
    for d in range(1, 16):
        d_copies.append(send(mine, mine, s_d.at[d], r_d.at[d], (peer(d), col)))
    e_copies.append(send(mine, mine, s_e.at[0], r_e.at[0], mate))
    for d in range(1, 16):
        d_copies[d - 1].wait_recv()
        came = gfull.at[piece(lax.rem(row + 16 - d, 16))]
        e_copies.append(send(came, came, s_e.at[d], r_e.at[d], mate))
    for d in (2, 1, 3):
        for h in range(2):
            first_steps(h, d).start()
            first(h, d).start()
    for copy in e_copies:
        copy.wait_recv()
    for i in range(1, 4):
        gsq[i, :, 0 : 128 * i] = jnp.zeros((128, 128 * i), F32)
    for n, (i, j) in enumerate(TRI):
        gsq[i, :, 128 * j : 128 * j + 128] = gfull[128 * n : 128 * n + 128, :]

    def between(k):
        @pl.when(k == MID)
        def _():
            for h in range(2):
                for d in range(1, 4):
                    first(h, d).wait_recv()
                    first_steps(h, d).wait_recv()

                for d in (2, 1, 3, 0):
                    e = lax.rem((py if h == 0 else px) + d, 4)
                    value = z_part(h, along(h, 0, e))
                    for f in range(1, 4):
                        value = value + zr1[h, f, e].astype(jnp.int32).astype(F32) * zu1[h, f, e]
                    if d == 0:
                        zown[h] = value
                    else:
                        pack(value, zs2, (h, d))
                        second(h, d).start()

    factor(gsq, x, w, between)

    def out_copy(there, here):
        return pltpu.make_async_remote_copy(
            src_ref=pbuf.at[pl.ds(pl.multiple_of(32 * there, 32), 32)], dst_ref=obuf.at[here],
            send_sem=s_o.at[there], recv_sem=r_o.at[here], device_id=(there, col), device_id_type=MESH,
        )

    for k in range(4):
        h = k // 2
        if k % 2 == 0:
            for d in range(1, 4):
                second(h, d).wait_recv()
            value = zown[h]
            for d in range(1, 4):
                step = step_of(zr2[h, d, 256:272, :])
                value = value + zr2[h, d, 0:256, :].astype(jnp.int32).astype(F32) * step
            if h == 1:
                for j in range(2):
                    value = value - dot_t(gsq[j, :, 256:512], pbuf[128 * j : 128 * j + 128, :])
            pbuf[256 * h : 256 * h + 256, :] = value
        solved = dot_hi(w[16 * k : 16 * k + 16].reshape(128, 128), pbuf[128 * k : 128 * k + 128, :])
        pbuf[128 * k : 128 * k + 128, :] = solved
        for there in range(4 * k, 4 * k + 4):

            @pl.when(row != there)
            def _():
                out_copy(there, row).start()

        if k % 2 == 0:
            after = slice(128 * k + 128, 128 * k + 256)
            pbuf[after, :] -= dot_t(gsq[k, :, after], solved)

    obuf[row] = pbuf[pl.ds(pl.multiple_of(32 * row, 32), 32), :]
    for d in range(1, 16):
        out_copy(row, peer(d)).wait_recv()
    for r in range(16):
        o_ref[:, 128 * r : 128 * r + 128] = obuf[r]
    for copy in mate_copies + part_copies + step_copies + full_copies + fwd_copies + c_copies + d_copies + e_copies:
        copy.wait_send()
    for there in range(16):

        @pl.when(row != there)
        def _():
            out_copy(there, row).wait_send()

    for h in range(2):
        for d in range(1, 4):
            first(h, d).wait_send()
            first_steps(h, d).wait_send()
            second(h, d).wait_send()


def shards(term_matrix, sign_bits, sampled):
    vmem = pl.BlockSpec(memory_space=pltpu.VMEM)
    dma = pltpu.SemaphoreType.DMA
    return pl.pallas_call(
        kernel,
        out_shape=jax.ShapeDtypeStruct((32, 2048), F32),
        in_specs=[pl.BlockSpec(memory_space=pl.ANY)] * 3,
        out_specs=vmem,
        scratch_shapes=[
            pltpu.VMEM((768, 2048), BF16),
            pltpu.VMEM((1, 2048), jnp.int32),
            pltpu.VMEM((16, 512), jnp.int32),
            pltpu.VMEM((2048, 512), BF16),
            pltpu.VMEM((2, 384, 256), F32),
            pltpu.VMEM((2, 384, 256), F32),
            pltpu.VMEM((2, 384, 256), F32),
            pltpu.VMEM((2, 8, 48, 256), jnp.int16),
            pltpu.VMEM((2, 8, 48, 256), jnp.int16),
            pltpu.VMEM((2, 1, 128), F32),
            pltpu.VMEM((2, 8, 1, 128), F32),
            pltpu.VMEM((2, 16, 48, 256), BF16),
            pltpu.VMEM((512, 768), BF16),
            pltpu.VMEM((1280, 128), F32),
            pltpu.VMEM((16, 40, 128), F32),
            pltpu.VMEM((1280, 128), F32),
            pltpu.VMEM((4, 128, 512), F32),
            pltpu.VMEM((32, 8, 128), F32),
            pltpu.VMEM((64, 8, 128), F32),
            pltpu.VMEM((512, 2048), F32),
            pltpu.VMEM((2, 4, 4, 256, 128), jnp.int16),
            pltpu.VMEM((2, 4, 4, 256, 128), jnp.int16),
            pltpu.VMEM((2, 4, 4, 1, 128), F32),
            pltpu.VMEM((2, 4, 4, 1, 128), F32),
            pltpu.VMEM((2, 4, 272, 128), jnp.int16),
            pltpu.VMEM((2, 4, 272, 128), jnp.int16),
            pltpu.VMEM((2, 256, 128), F32),
            pltpu.VMEM((512, 128), F32),
            pltpu.VMEM((16, 32, 128), F32),
            dma((4,)),
        ]
        + [dma((2,))] * 2
        + [dma((2, 8))] * 8
        + [dma((16,))] * 6
        + [dma((2, 4))] * 6
        + [dma((16,))] * 2,
        compiler_params=pltpu.CompilerParams(collective_id=0, has_side_effects=True, vmem_limit_bytes=60 << 20),
    )(term_matrix, sign_bits.reshape(1, 2048), sampled)


def solution(mesh):
    in_specs = (P("row", "col"), P("col"), P("col", None))
    return jax.shard_map(shards, mesh=mesh, in_specs=in_specs, out_specs=P("row", "col"), check_vma=False)
```

```python
import jax
import jax.numpy as jnp
from jax import lax
from jax.experimental import pallas as pl
from jax.experimental.pallas import tpu as pltpu
from jax.sharding import PartitionSpec as P

MESH = pl.DeviceIdType.MESH
F32 = jnp.float32
BF16 = jnp.bfloat16
STRIPS = 4
LN2 = 0.6931471805599453


def barrier(targets):
    sem = pltpu.get_barrier_semaphore()
    for target in targets:
        pl.semaphore_signal(sem, inc=1, device_id=target, device_id_type=MESH)
    return lambda: pl.semaphore_wait(sem, len(targets))


def send(src, dst, send_sem, recv_sem, target):
    copy = pltpu.make_async_remote_copy(
        src_ref=src, dst_ref=dst, send_sem=send_sem, recv_sem=recv_sem, device_id=target, device_id_type=MESH
    )
    copy.start()
    return copy


def power_of(value):
    top = jnp.max(jnp.max(jnp.abs(value), axis=0, keepdims=True), axis=1, keepdims=True)
    return jnp.ceil(jnp.log(jnp.maximum(top, 1e-30)) * (1.0 / LN2)) - 14.0


def coded(value, power):
    return jnp.floor(value * jnp.exp(power * -LN2) + 0.5).astype(jnp.int32).astype(jnp.int16)


def pack(value, ref, at):
    power = power_of(value)
    ref[at + (slice(0, 256),)] = coded(value, power)
    ref[at + (slice(256, 272),)] = jnp.broadcast_to(power, (16, 128)).astype(jnp.int32).astype(jnp.int16)


def step_of(power):
    return jnp.exp(power.astype(jnp.int32).astype(F32) * LN2)[0:1, :]


AHEAD = 2


def lane_of(x, lane):
    return jnp.broadcast_to(x[:, lane : lane + 1], (8, 128))


def split(u):
    high = u.astype(BF16)
    return high, (u - high.astype(F32)).astype(BF16)


def dot_t(a, b):
    ah, am = split(a)
    bh, bm = split(b)
    left = jnp.concatenate([ah, ah, am], 0)
    right = jnp.concatenate([bh, bm, bh], 0)
    return lax.dot_general(left, right, (((0,), (0,)), ((), ())), preferred_element_type=F32)


def dot_hi(a, b):
    ah, am = split(a)
    bh, bm = split(b)
    left = jnp.concatenate([ah, ah, am], 1)
    right = jnp.concatenate([bh, bm, bh], 0)
    return jnp.dot(left, right, preferred_element_type=F32)


def factor_block(x, w, base):
    lanes = lax.broadcasted_iota(jnp.int32, (8, 128), 1)
    for t in range(16):
        at = 8 * t
        strip = x[t]
        for j in range(8):
            x[24 + j] = lane_of(strip, at + j)
        here = (lanes >= at) & (lanes < at + 8)
        a = [[None] * 8 for _ in range(8)]
        for i in range(8):
            for j in range(i, 8):
                a[i][j] = jnp.broadcast_to(x[24 + j, i : i + 1, :], (8, 128))
        rows = [jnp.where(here, (lanes == at + i).astype(F32), jnp.broadcast_to(x[t, i : i + 1, :], (8, 128))) for i in range(8)]
        recips, mult = [], [[None] * 8 for _ in range(8)]
        for k in range(8):
            recips.append(1.0 / a[k][k])
            for j in range(k + 1, 8):
                mult[k][j] = a[k][j] * recips[k]
            for i in range(k + 1, 8):
                for j in range(i, 8):
                    a[i][j] = a[i][j] - mult[k][i] * a[k][j]
            for j in range(k + 1, 8):
                rows[j] = rows[j] - mult[k][j] * rows[k]
        last = STRIPS * (t // STRIPS) + STRIPS
        reach = min(last + AHEAD, 16)
        done = lanes < at + 8
        for k in range(8):
            u = rows[k] * lax.rsqrt(a[k][k])
            w[base // 8 + t, k : k + 1, :] = jnp.where(done, u, 0.0)[0:1]
            if reach < 16:
                x[16 + t % STRIPS, k : k + 1, :] = jnp.where(done | (lanes >= 8 * last), u, 0.0)[0:1]
        scaled = [rows[k] * recips[k] for k in range(8)]
        for s in range(t + 1, reach):
            old = x[s]
            new = jnp.where(here, 0.0, old)
            c = [lane_of(old, at + k) for k in range(8)]
            for k in range(8):
                for j in range(k):
                    c[k] = c[k] - c[j] * mult[j][k]
                new = new - c[k] * scaled[k]
            x[s] = new
        if t + 1 == last and reach < 16:
            u = x[16 : 16 + STRIPS].reshape(8 * STRIPS, 128)
            change = dot_t(u, u)[8 * reach :].reshape(16 - reach, 8, 128)
            inside = (lanes >= 8 * (last - STRIPS)) & (lanes < 8 * last)
            x[reach:16] = jnp.where(inside[None], 0.0, x[reach:16]) - change


def factor(g, x, w, between):
    def step(k, carry):
        between(k)
        x[0:16] = g[k, :, pl.ds(pl.multiple_of(128 * k, 128), 128)].reshape(16, 8, 128)
        factor_block(x, w, 128 * k)

        @pl.when(k < 3)
        def _():
            panel = dot_hi(w[pl.ds(16 * k, 16)].reshape(128, 128), g[k])
            g[k] = panel
            change = dot_t(panel, panel)
            for i in range(1, 4):

                @pl.when(i > k)
                def _():
                    g[i] = g[i] - change[128 * i : 128 * i + 128]

        return carry

    lax.fori_loop(0, 4, step, 0)


TRI = [(i, j) for i in range(4) for j in range(i, 4)]
FAR_FIRST = (4, 3, 5, 2, 6, 1, 7)
NEAR_FIRST = FAR_FIRST[::-1]
MID = 3


def kernel(
    a_hbm, sign_hbm, samp_hbm, o_ref,
    a, sign_ref, samp_ref, om, mate_out, mate_in, own, part_out, part_in, step_out, step_in, full, yt, gloc, gin, gfull, gsq, x, w,
    zf, zs1, zr1, zt1, zu1, zs2, zr2, zown, pbuf, obuf,
    s_a, s_mate, r_mate, s_part, r_part, s_step, r_step, s_full, r_full, s_fwd, r_fwd,
    s_c, r_c, s_d, r_d, s_e, r_e, s_z1, r_z1, s_t1, r_t1, s_z2, r_z2, s_o, r_o,
):
    row, col = lax.axis_index("row"), lax.axis_index("col")
    z, core = col // 2, lax.rem(col, 2)
    py, px = row // 4, lax.rem(row, 4)
    mate = (row, 2 * z + 1 - core)

    def chip(distance):
        return (row, 2 * lax.rem(z + distance, 8) + core)

    def peer(d):
        return lax.rem(row + d, 16)

    def half_rows(which):
        return pl.ds(pl.multiple_of(which * 384, 384), 384)

    small = [
        pltpu.make_async_copy(samp_hbm, samp_ref, s_a.at[2]),
        pltpu.make_async_copy(sign_hbm, sign_ref, s_a.at[3]),
    ]
    for load in small:
        load.start()
    loads = []
    for n, which in enumerate((1 - core, core)):
        loads.append(pltpu.make_async_copy(a_hbm.at[half_rows(which)], a.at[half_rows(which)], s_a.at[n]))
        loads[n].start()
    ready = barrier([mate] + [chip(d) for d in range(1, 8)] + [(peer(d), col) for d in range(1, 16)])

    for load in small:
        load.wait()

    term = lax.broadcasted_iota(jnp.int32, (128, 512), 0)
    for block in range(16):
        parity = lax.population_count(term & samp_ref[block : block + 1, :]) & 1
        om[128 * block : 128 * block + 128, :] = (1 - 2 * parity).astype(F32).astype(BF16)
    signs = (2 * sign_ref[...] - 1).astype(F32).astype(BF16)

    def partial(which, n):
        rows = a[half_rows(which), :] * signs
        return jnp.dot(rows, om[:, 256 * n : 256 * n + 256], preferred_element_type=F32)

    mate_copies, part_copies, step_copies, full_copies, fwd_copies = [], [], [], [], []
    loads[0].wait()
    for n in range(2):
        mate_out[n] = partial(1 - core, n)
        if n == 0:
            ready()
        mate_copies.append(send(mate_out.at[n], mate_in.at[n], s_mate.at[n], r_mate.at[n], mate))
    loads[1].wait()
    for n in range(2):
        own[n] = partial(core, n)
        mate_copies[n].wait_recv()
        own[n] += mate_in[n]
        power = power_of(own[n])
        step_out[n] = jnp.broadcast_to(jnp.exp(power * LN2), (1, 128))
        for d in FAR_FIRST:
            there = lax.rem(z + d, 8)
            part_out[n, d] = coded(own[n, pl.ds(pl.multiple_of(there * 48, 48), 48), :], power)
            part_copies.append(send(part_out.at[n, d], part_in.at[n, d], s_part.at[n, d], r_part.at[n, d], chip(d)))
            step_copies.append(send(step_out.at[n], step_in.at[n, d], s_step.at[n, d], r_step.at[n, d], chip(d)))
    slot = core * 8 + z
    for n in range(2):
        for copy in part_copies[7 * n : 7 * n + 7] + step_copies[7 * n : 7 * n + 7]:
            copy.wait_recv()
        for j in range(2):
            half = slice(128 * j, 128 * j + 128)
            total = own[n, pl.ds(pl.multiple_of(z * 48, 48), 48), half]
            for d in range(1, 8):
                total = total + part_in[n, d, :, half].astype(jnp.int32).astype(F32) * step_in[n, d]
            full[n, slot, :, half] = total.astype(BF16)
        mine = full.at[n, slot]
        for d in FAR_FIRST:
            full_copies.append(send(mine, mine, s_full.at[n, d], r_full.at[n, d], chip(d)))
        fwd_copies.append(send(mine, mine, s_fwd.at[n, 0], r_fwd.at[n, 0], mate))
    def piece(r):
        return pl.ds(pl.multiple_of(40 * (2 * r + core), 8), 40)

    def gram(i, n):
        blocks = jnp.dot(yt[128 * i : 128 * i + 128, :], full[n].reshape(768, 256), preferred_element_type=F32)
        for j in range(2 * n, 2 * n + 2):
            if j >= i:
                at = 128 * TRI.index((i, j))
                gloc[at : at + 128, :] = blocks[:, 128 * (j - 2 * n) : 128 * (j - 2 * n) + 128]

    def product(h):
        def columns(m, carry):
            cols = pl.ds(pl.multiple_of(256 * m, 256), 256)
            zf[256 * h : 256 * h + 256, cols] = jnp.dot(yt[256 * h : 256 * h + 256, :], a[:, cols], preferred_element_type=F32)
            return carry

        lax.fori_loop(0, 8, columns, 0)

    c_copies, d_copies, e_copies = [], [], []
    for n in range(2):
        for m, d in enumerate(FAR_FIRST):
            full_copies[7 * n + m].wait_recv()
            came = full.at[n, core * 8 + lax.rem(z + 8 - d, 8)]
            fwd_copies.append(send(came, came, s_fwd.at[n, d], r_fwd.at[n, d], mate))
        if n == 1:
            product(0)
        for copy in fwd_copies[n : n + 1] + fwd_copies[2 + 7 * n : 9 + 7 * n]:
            copy.wait_recv()
        for i in range(2 * n, 2 * n + 2):
            yt[128 * i : 128 * i + 128, :] = full[n, :, :, 128 * (i % 2) : 128 * (i % 2) + 128].reshape(768, 128).T
        for i in range(2 * n + 2):
            gram(i, n)
    for d in range(1, 16):
        c_copies.append(send(gloc.at[piece(peer(d))], gin.at[d], s_c.at[d], r_c.at[d], (peer(d), col)))
    product(1)

    def along(h, d, e):
        return (4 * e + lax.rem(px + d, 4)) if h == 0 else (4 * lax.rem(py + d, 4) + e)

    def first(h, d):
        target = (along(h, d, py if h == 0 else px), col)
        return pltpu.make_async_remote_copy(
            src_ref=zs1.at[h, d], dst_ref=zr1.at[h, d], send_sem=s_z1.at[h, d], recv_sem=r_z1.at[h, d], device_id=target, device_id_type=MESH
        )

    def first_steps(h, d):
        target = (along(h, d, py if h == 0 else px), col)
        return pltpu.make_async_remote_copy(
            src_ref=zt1.at[h, d], dst_ref=zu1.at[h, d], send_sem=s_t1.at[h, d], recv_sem=r_t1.at[h, d], device_id=target, device_id_type=MESH
        )

    def second(h, d):
        target = (along(1 - h, d, px if h == 0 else py), col)
        return pltpu.make_async_remote_copy(
            src_ref=zs2.at[h, d], dst_ref=zr2.at[h, d], send_sem=s_z2.at[h, d], recv_sem=r_z2.at[h, d], device_id=target, device_id_type=MESH
        )

    def z_part(h, r):
        return zf[256 * h : 256 * h + 256, pl.ds(pl.multiple_of(128 * r, 128), 128)]

    for h in range(2):

        def code(m, carry):
            d, e = m // 4 + 1, lax.rem(m, 4)
            value = z_part(h, along(h, d, e))
            power = power_of(value)
            zs1[h, d, e] = coded(value, power)
            zt1[h, d, e] = jnp.broadcast_to(jnp.exp(power * LN2), (1, 128))
            return carry

        lax.fori_loop(0, 12, code, 0)

    for copy in mate_copies + part_copies + step_copies + full_copies + fwd_copies:
        copy.wait_send()
    for i in range(1, 4):
        gsq[i, :, 0 : 128 * i] = jnp.zeros((128, 128 * i), F32)
    for copy in c_copies:
        copy.wait_recv()
    total = gloc[piece(row), :]
    for d in range(1, 16):
        total = total + gin[d]
    gfull[piece(row), :] = total
    mine = gfull.at[piece(row)]
    for d in range(1, 16):
        d_copies.append(send(mine, mine, s_d.at[d], r_d.at[d], (peer(d), col)))
    e_copies.append(send(mine, mine, s_e.at[0], r_e.at[0], mate))
    for copy in c_copies:
        copy.wait_send()
    for d in range(1, 16):
        d_copies[d - 1].wait_recv()
        came = gfull.at[piece(lax.rem(row + 16 - d, 16))]
        e_copies.append(send(came, came, s_e.at[d], r_e.at[d], mate))
    for d in (2, 1, 3):
        for h in range(2):
            first_steps(h, d).start()
            first(h, d).start()
    for copy in e_copies:
        copy.wait_recv()
    for n, (i, j) in enumerate(TRI):
        gsq[i, :, 128 * j : 128 * j + 128] = gfull[128 * n : 128 * n + 128, :]

    def between(k):
        @pl.when(k == MID)
        def _():
            for h in range(2):
                for d in range(1, 4):
                    first(h, d).wait_recv()
                    first_steps(h, d).wait_recv()

                for d in (2, 1, 3, 0):
                    e = lax.rem((py if h == 0 else px) + d, 4)
                    value = z_part(h, along(h, 0, e))
                    for f in range(1, 4):
                        value = value + zr1[h, f, e].astype(jnp.int32).astype(F32) * zu1[h, f, e]
                    if d == 0:
                        zown[h] = value
                    else:
                        pack(value, zs2, (h, d))
                        second(h, d).start()

    factor(gsq, x, w, between)
    for copy in d_copies + e_copies:
        copy.wait_send()
    for h in range(2):
        for d in range(1, 4):
            first(h, d).wait_send()
            first_steps(h, d).wait_send()

    def out_copy(there, here):
        return pltpu.make_async_remote_copy(
            src_ref=pbuf.at[pl.ds(pl.multiple_of(32 * there, 32), 32)], dst_ref=obuf.at[here],
            send_sem=s_o.at[there], recv_sem=r_o.at[here], device_id=(there, col), device_id_type=MESH,
        )

    for k in range(4):
        h = k // 2
        if k % 2 == 0:
            for d in range(1, 4):
                second(h, d).wait_recv()
            value = zown[h]
            for d in range(1, 4):
                step = step_of(zr2[h, d, 256:272, :])
                value = value + zr2[h, d, 0:256, :].astype(jnp.int32).astype(F32) * step
            if h == 1:
                for j in range(2):
                    value = value - dot_t(gsq[j, :, 256:512], pbuf[128 * j : 128 * j + 128, :])
            pbuf[256 * h : 256 * h + 256, :] = value
        solved = dot_hi(w[16 * k : 16 * k + 16].reshape(128, 128), pbuf[128 * k : 128 * k + 128, :])
        pbuf[128 * k : 128 * k + 128, :] = solved
        for there in range(4 * k, 4 * k + 4):

            @pl.when(row != there)
            def _():
                out_copy(there, row).start()

        if k % 2 == 0:
            after = slice(128 * k + 128, 128 * k + 256)
            pbuf[after, :] -= dot_t(gsq[k, :, after], solved)

    obuf[row] = pbuf[pl.ds(pl.multiple_of(32 * row, 32), 32), :]
    for d in range(1, 16):
        out_copy(row, peer(d)).wait_recv()
    for r in range(16):
        o_ref[:, 128 * r : 128 * r + 128] = obuf[r]
    for there in range(16):

        @pl.when(row != there)
        def _():
            out_copy(there, row).wait_send()

    for h in range(2):
        for d in range(1, 4):
            second(h, d).wait_send()


def shards(term_matrix, sign_bits, sampled):
    vmem = pl.BlockSpec(memory_space=pltpu.VMEM)
    dma = pltpu.SemaphoreType.DMA
    return pl.pallas_call(
        kernel,
        out_shape=jax.ShapeDtypeStruct((32, 2048), F32),
        in_specs=[pl.BlockSpec(memory_space=pl.ANY)] * 3,
        out_specs=vmem,
        scratch_shapes=[
            pltpu.VMEM((768, 2048), BF16),
            pltpu.VMEM((1, 2048), jnp.int32),
            pltpu.VMEM((16, 512), jnp.int32),
            pltpu.VMEM((2048, 512), BF16),
            pltpu.VMEM((2, 384, 256), F32),
            pltpu.VMEM((2, 384, 256), F32),
            pltpu.VMEM((2, 384, 256), F32),
            pltpu.VMEM((2, 8, 48, 256), jnp.int16),
            pltpu.VMEM((2, 8, 48, 256), jnp.int16),
            pltpu.VMEM((2, 1, 128), F32),
            pltpu.VMEM((2, 8, 1, 128), F32),
            pltpu.VMEM((2, 16, 48, 256), BF16),
            pltpu.VMEM((512, 768), BF16),
            pltpu.VMEM((1280, 128), F32),
            pltpu.VMEM((16, 40, 128), F32),
            pltpu.VMEM((1280, 128), F32),
            pltpu.VMEM((4, 128, 512), F32),
            pltpu.VMEM((32, 8, 128), F32),
            pltpu.VMEM((64, 8, 128), F32),
            pltpu.VMEM((512, 2048), F32),
            pltpu.VMEM((2, 4, 4, 256, 128), jnp.int16),
            pltpu.VMEM((2, 4, 4, 256, 128), jnp.int16),
            pltpu.VMEM((2, 4, 4, 1, 128), F32),
            pltpu.VMEM((2, 4, 4, 1, 128), F32),
            pltpu.VMEM((2, 4, 272, 128), jnp.int16),
            pltpu.VMEM((2, 4, 272, 128), jnp.int16),
            pltpu.VMEM((2, 256, 128), F32),
            pltpu.VMEM((512, 128), F32),
            pltpu.VMEM((16, 32, 128), F32),
            dma((4,)),
        ]
        + [dma((2,))] * 2
        + [dma((2, 8))] * 8
        + [dma((16,))] * 6
        + [dma((2, 4))] * 6
        + [dma((16,))] * 2,
        compiler_params=pltpu.CompilerParams(collective_id=0, has_side_effects=True, vmem_limit_bytes=60 << 20),
    )(term_matrix, sign_bits.reshape(1, 2048), sampled)


def solution(mesh):
    in_specs = (P("row", "col"), P("col"), P("col", None))
    return jax.shard_map(shards, mesh=mesh, in_specs=in_specs, out_specs=P("row", "col"), check_vma=False)
```
